32 devices in a mesh: dp: 8 (over z, core), tensor: 4 (over y, x).
Axes of the slice: x: 2, y: 2, z: 4, core: 2. Of those that a mesh axis runs over, the one named last changes fastest.
Arguments:
- history: bfloat16 [4, 1536, 4096], P(None, 'dp'), may hold values from -6 to 6
- depth_weights: float32 [4], replicated, may hold values from 0.2 to 1
- depth_index: int32 [4], replicated, may hold values from 0 to 3
- gain: float32 [4096], replicated, may hold values from 0.1 to 1.9
- gate_blocks: bfloat16 [896, 128, 128], P(('tensor', 'dp')), may hold values from -0.1875 to 0.1875
- up_blocks: bfloat16 [896, 128, 128], P(('tensor', 'dp')), may hold values from -0.1875 to 0.1875
- down_blocks: bfloat16 [896, 128, 128], P(('tensor', 'dp')), may hold values from -0.09375 to 0.09375
- block_ids: int32 [896, 2], P('tensor'), may hold values from 0 to 31, as said below
- grad_out: bfloat16 [1536, 4096], P('dp'), may hold values from -16 to 16
Outputs:
- layer_out: bfloat16 [1536, 4096], P('dp', 'tensor')
- grad_mixed: float32 [1536, 4096], P('dp', 'tensor')
- grad_gate: float32 [896, 128, 128], P(('tensor', 'dp'))
- grad_up: float32 [896, 128, 128], P(('tensor', 'dp'))
- grad_down: float32 [896, 128, 128], P(('tensor', 'dp'))
- grad_depth: float32 [4], replicated
- grad_gain: float32 [4096], P('tensor')
The draws below stay inside these ranges and needn't reach their ends.
Inputs may be any that keep to these rules, and one draw needn't show every extreme that they name: `block_ids`: within the 224 rows of one index of tensor the pairs are distinct; column 0 is a row block below 32, column 1 a column block below 28 counted within that index's hidden units.
All inputs are finite; a program needn't handle non-finite values.
Results may differ from the reference program's by a relative error of at most 0.025.
Values may be sent and summed in bfloat16 or wider, within the bound.
A program may use at most 192 MiB of HBM per device.

```python
import jax
import jax.numpy as jnp
from jax import lax

D = 4096
FF = 14336
BS = 128
HIST = 4
NW = 4
TOK_DEV = 192
TOKENS = 1536
RB = 32
HB = 28
NBLK_SH = 224
NBLK = 896
N_DP = 8
N_TENSOR = 4


def draw_block_ids(key, part):
    shards = NBLK // NBLK_SH
    subkeys = jax.random.split(key, shards)

    def choose_shard(subkey):
        return jax.random.permutation(subkey, RB * HB)[:NBLK_SH]
    chosen = jax.vmap(choose_shard)(subkeys).reshape(NBLK).astype(jnp.int32)
    return jnp.stack([chosen // HB, chosen % HB], axis=1).astype(jnp.int32)


def draw_grad_out(key, part):
    position = jnp.arange(TOKENS, dtype=jnp.float32) / (TOKENS - 1)
    values = jnp.clip(jax.random.normal(key, (TOKENS, D), jnp.float32), -4.0, 4.0)
    values = values * (1.0 + 2.0 * position)[:, None]
    return values.astype(jnp.bfloat16)


def plant(result, own_key, low, top_value):
    longest = result.shape.index(max(result.shape))
    spots = []
    for shift in (0, 1):
        where = [jax.random.randint(jax.random.fold_in(own_key, axis), (), 0, length) for axis, length in enumerate(result.shape)]
        where[longest] = (where[longest] + shift) % result.shape[longest]
        spots.append(tuple(where))
    return result.at[spots[0]].set(low).at[spots[1]].set(top_value)


def shard_levels(own_key, shape, cuts, low, top_value):
    factor_of, own = 1.0, jax.random.fold_in(own_key, 6)
    for dim, shards_of in cuts:
        draws = jnp.exp(jax.random.uniform(jax.random.fold_in(own, dim), (shards_of,), jnp.float32, low / len(cuts), top_value / len(cuts)))
        factor_of = factor_of * jnp.repeat(draws, shape[dim] // shards_of).reshape([-1 if axis == dim else 1 for axis in range(len(shape))])
    return factor_of


def scatter_about(rng, extent, deviation, limit, cuts=(), held_as=jnp.bfloat16):
    factor_of = shard_levels(rng, extent, cuts, -0.22, 0.18) if cuts else 1.0
    values = jax.random.normal(rng, extent, jnp.float32) * deviation * factor_of
    return jnp.minimum(jnp.maximum(values, -limit), limit).astype(held_as)


def setup_inputs(seed: int = 0) -> dict:
    splits = jax.random.split(jax.random.key(seed), 10)
    history = scatter_about(splits[0], (HIST, TOKENS, D), 1.0, 6.0, ((1, 8),))
    depth_weights = jnp.clip(jax.random.uniform(splits[1], (NW,), jnp.float32, 0.2, 1.0), 0.2, 1.0)
    depth_index = plant(jax.random.randint(splits[2], (NW,), 0, HIST), jax.random.fold_in(splits[2], 1), 0, HIST - 1).astype(jnp.int32)
    gain = jnp.clip(1.0 + 0.18 * jax.random.normal(splits[3], (D,), jnp.float32), 0.1, 1.9)
    gate_blocks = scatter_about(splits[4], (NBLK, BS, BS), (D // 4) ** -0.5, 0.1875, ((0, 32),))
    up_blocks = scatter_about(splits[5], (NBLK, BS, BS), (D // 4) ** -0.5, 0.1875, ((0, 32),))
    down_blocks = scatter_about(splits[6], (NBLK, BS, BS), (FF // 4) ** -0.5, 0.09375, ((0, 32),))
    block_ids = draw_block_ids(jax.random.fold_in(splits[9], 71), 0)
    grad_out = draw_grad_out(jax.random.fold_in(splits[9], 71), 0)
    return dict(history=history, depth_weights=depth_weights, depth_index=depth_index, gain=gain, gate_blocks=gate_blocks, up_blocks=up_blocks, down_blocks=down_blocks, block_ids=block_ids, grad_out=grad_out)


EPSILON = 1e-05

def norm_rows(mixed, gain):
    scale_inv = lax.rsqrt(lax.optimization_barrier(jnp.mean(mixed * mixed, axis=-1, keepdims=True)) + EPSILON)
    return mixed * scale_inv * gain

def group_sum(left_rows, right_rows):
    left_groups = left_rows.astype(jnp.float32).reshape(N_DP, TOK_DEV, -1, BS)
    right_groups = right_rows.astype(jnp.float32).reshape(N_DP, TOK_DEV, -1, BS)
    partial_terms = jnp.einsum('gtbi,gtbj->gbij', left_groups, right_groups)
    rounded = lax.optimization_barrier(partial_terms.astype(jnp.bfloat16))
    return lax.optimization_barrier(jnp.sum(rounded.astype(jnp.float32), axis=0))

def reference(history, depth_weights, depth_index, gain, gate_blocks, up_blocks, down_blocks, block_ids, grad_out):
    mixed = jnp.zeros((TOKENS, D), jnp.float32)
    for layer_slot in range(NW):
        earlier = lax.dynamic_index_in_dim(history, depth_index[layer_slot], 0, keepdims=False)
        mixed = mixed + depth_weights[layer_slot] * earlier.astype(jnp.float32)
    normed = norm_rows(mixed, gain).astype(jnp.bfloat16)
    normed3 = normed.reshape(TOKENS, RB, BS)
    out3 = grad_out.reshape(TOKENS, RB, BS)
    shard_pairs = block_ids.reshape(N_TENSOR, NBLK_SH, 2)
    gate_shards = gate_blocks.reshape(N_TENSOR, NBLK_SH, BS, BS)
    up_shards = up_blocks.reshape(N_TENSOR, NBLK_SH, BS, BS)
    down_shards = down_blocks.reshape(N_TENSOR, NBLK_SH, BS, BS)

    def hidden_parts(row_ids, col_ids, gate_w, up_w):
        picked = jnp.take(normed3, row_ids, axis=1).astype(jnp.float32)
        zero_cols = jnp.zeros((TOKENS, HB, BS), jnp.float32)
        gate = zero_cols.at[:, col_ids].add(jnp.einsum('tbi,bij->tbj', picked, gate_w.astype(jnp.float32)))
        up = zero_cols.at[:, col_ids].add(jnp.einsum('tbi,bij->tbj', picked, up_w.astype(jnp.float32)))
        hidden = (jax.nn.silu(gate) * up).astype(jnp.bfloat16)
        return (gate, up, hidden)

    def forward_step(totals, shard_data):
        block_pairs, gate_w, up_w, down_w = shard_data
        row_ids = block_pairs[:, 0]
        col_ids = block_pairs[:, 1]
        gate, up, hidden = hidden_parts(row_ids, col_ids, gate_w, up_w)
        picked = jnp.take(hidden, col_ids, axis=1).astype(jnp.float32)
        totals = totals.at[:, row_ids].add(jnp.einsum('tbi,bij->tbj', picked, down_w.astype(jnp.float32)))
        return (totals, None)
    zero_rows = jnp.zeros((TOKENS, RB, BS), jnp.float32)
    ffn3, unused = lax.scan(forward_step, zero_rows, (shard_pairs, gate_shards, up_shards, down_shards))
    layer_out = (mixed + ffn3.reshape(TOKENS, D)).astype(jnp.bfloat16)

    def backward_step(totals, shard_data):
        block_pairs, gate_w, up_w, down_w = shard_data
        row_ids = block_pairs[:, 0]
        col_ids = block_pairs[:, 1]
        gate, up, hidden = hidden_parts(row_ids, col_ids, gate_w, up_w)
        out_rows = jnp.take(out3, row_ids, axis=1)
        zero_cols = jnp.zeros((TOKENS, HB, BS), jnp.float32)
        grad_hidden = zero_cols.at[:, col_ids].add(jnp.einsum('tbj,bij->tbi', out_rows.astype(jnp.float32), down_w.astype(jnp.float32)))
        sigmoid_gate = jax.nn.sigmoid(gate)
        grad_gate_pre = (grad_hidden * up * sigmoid_gate * (1.0 + gate * (1.0 - sigmoid_gate))).astype(jnp.bfloat16)
        grad_up_pre = (grad_hidden * gate * sigmoid_gate).astype(jnp.bfloat16)
        gate_cols = jnp.take(grad_gate_pre, col_ids, axis=1)
        up_cols = jnp.take(grad_up_pre, col_ids, axis=1)
        contrib = jnp.einsum('tbj,bij->tbi', gate_cols.astype(jnp.float32), gate_w.astype(jnp.float32))
        contrib = contrib + jnp.einsum('tbj,bij->tbi', up_cols.astype(jnp.float32), up_w.astype(jnp.float32))
        totals = totals.at[:, row_ids].add(contrib)
        in_rows = jnp.take(normed3, row_ids, axis=1)
        hidden_cols = jnp.take(hidden, col_ids, axis=1)
        block_grads = jnp.stack([group_sum(in_rows, gate_cols), group_sum(in_rows, up_cols), group_sum(hidden_cols, out_rows)], axis=1)
        return (totals, block_grads)
    grad_normed3, block_grads = lax.scan(backward_step, zero_rows, (shard_pairs, gate_shards, up_shards, down_shards))
    block_grads = block_grads.reshape(NBLK, 3, BS, BS)
    grad_normed = grad_normed3.reshape(TOKENS, D)
    ignored, pull_back = jax.vjp(norm_rows, mixed, gain)
    grad_x, grad_gain = pull_back(grad_normed)
    grad_mixed = grad_out.astype(jnp.float32) + grad_x
    depth_list = []
    for layer_slot in range(NW):
        earlier = lax.dynamic_index_in_dim(history, depth_index[layer_slot], 0, keepdims=False)
        depth_list.append(jnp.sum(grad_mixed * earlier.astype(jnp.float32)))
    grad_depth = jnp.stack(depth_list)
    return (layer_out, grad_mixed, block_grads[:, 0], block_grads[:, 1], block_grads[:, 2], grad_depth, grad_gain)
```

```python
import functools

import jax
import jax.numpy as jnp
from jax import lax
from jax.experimental import pallas as pl
from jax.experimental.pallas import tpu as pltpu
from jax.sharding import PartitionSpec as P

FF = 14336
EPSILON = 1e-05
CHUNKS = 8
UNROLL = 7
F32 = jnp.float32
BF16 = jnp.bfloat16
NN = (((1,), (0,)), ((), ()))
NT = (((1,), (1,)), ((), ()))
TN = (((0,), (0,)), ((), ()))


def dot(a, b, dims):
    return lax.dot_general(a, b, dims, preferred_element_type=F32)


def lanes(index, size):
    return pl.ds(pl.multiple_of(index * size, size), size)


def for_blocks(ids, first, count, body):
    def step(i, carry):
        for u in range(UNROLL):
            b = i * UNROLL + u
            body(b, ids[2 * (first + b)], ids[2 * (first + b) + 1])
        return carry

    lax.fori_loop(0, count // UNROLL, step, 0)


def for_columns(size, width, body):
    def step(c, carry):
        body(lanes(c, size))
        return carry

    lax.fori_loop(0, width // size, step, 0)


def gate_kernel(ids, x, w, acc):
    n, size = w.shape[0], w.shape[1]

    @pl.when(pl.program_id(0) == 0)
    def _():
        acc[...] = jnp.zeros_like(acc)

    def body(b, r, c):
        acc[:, lanes(c, size)] += dot(x[:, lanes(r, size)], w[b], NN)

    for_blocks(ids, pl.program_id(0) * n, n, body)


def up_kernel(ids, x, w, gate, acc, hidden):
    n, size = w.shape[0], w.shape[1]
    gate_kernel(ids, x, w, acc)

    @pl.when(pl.program_id(0) == pl.num_programs(0) - 1)
    def _():
        def body(cols):
            g = gate[:, cols]
            hidden[:, cols] = (g / (1.0 + jnp.exp(-g)) * acc[:, cols]).astype(BF16)

        for_columns(size, acc.shape[1], body)


def hidden_grad_kernel(ids, gout, w, gate, up, dgate, dup, acc):
    n, size = w.shape[0], w.shape[1]

    @pl.when(pl.program_id(0) == 0)
    def _():
        acc[...] = jnp.zeros_like(acc)

    def body(b, r, c):
        acc[:, lanes(c, size)] += dot(gout[:, lanes(r, size)], w[b], NT)

    for_blocks(ids, pl.program_id(0) * n, n, body)

    @pl.when(pl.program_id(0) == pl.num_programs(0) - 1)
    def _():
        def finish(cols):
            g = gate[:, cols]
            s = 1.0 / (1.0 + jnp.exp(-g))
            gh = acc[:, cols]
            dgate[:, cols] = (gh * up[:, cols] * s * (1.0 + g * (1.0 - s))).astype(BF16)
            dup[:, cols] = (gh * g * s).astype(BF16)

        for_columns(size, acc.shape[1], finish)


def ffn_kernel(ids, hidden, w, out, acc):
    n, size = w.shape[0], w.shape[1]

    @pl.when(pl.program_id(0) == 0)
    def _():
        acc[...] = jnp.zeros_like(acc)

    def body(b, r, c):
        acc[:, lanes(r, size)] += dot(hidden[:, lanes(c, size)], w[b], NN)

    for_blocks(ids, pl.program_id(0) * n, n, body)

    @pl.when(pl.program_id(0) == pl.num_programs(0) - 1)
    def _():
        out[...] = acc[...].astype(BF16)


def normed_grad_kernel(ids, dgate, dup, gate_w, up_w, out, acc):
    n, size = gate_w.shape[0], gate_w.shape[1]

    @pl.when(pl.program_id(0) == 0)
    def _():
        acc[...] = jnp.zeros_like(acc)

    def body(b, r, c):
        left = jnp.concatenate([dgate[:, lanes(c, size)], dup[:, lanes(c, size)]], axis=1)
        right = jnp.concatenate([gate_w[b], up_w[b]], axis=1)
        acc[:, lanes(r, size)] += dot(left, right, NT)

    for_blocks(ids, pl.program_id(0) * n, n, body)

    @pl.when(pl.program_id(0) == pl.num_programs(0) - 1)
    def _():
        out[...] = acc[...].astype(BF16)


def down_grad_kernel(ids, hidden, gout, out):
    n, size = out.shape[0], out.shape[1]

    def body(b, r, c):
        out[b] = dot(hidden[:, lanes(c, size)], gout[:, lanes(r, size)], TN).astype(BF16)

    for_blocks(ids, pl.program_id(0) * n, n, body)


def gate_up_grad_kernel(ids, x, dgate, dup, out_gate, out_up):
    n, size = out_gate.shape[0], out_gate.shape[1]

    def body(b, r, c):
        right = jnp.concatenate([dgate[:, lanes(c, size)], dup[:, lanes(c, size)]], axis=1)
        both = dot(x[:, lanes(r, size)], right, TN).astype(BF16)
        out_gate[b] = both[:, :size]
        out_up[b] = both[:, size:]

    for_blocks(ids, pl.program_id(0) * n, n, body)


def call(kernel, ids, whole, blocks, outs, flops, steps, acc=None, name=None):
    chunked = lambda shape: pl.BlockSpec((shape[0] // steps, *shape[1:]), lambda i, ids: (i, 0, 0))
    resident = lambda shape: pl.BlockSpec(shape, lambda i, ids: (0, 0))
    order = [(a, resident(a.shape)) if a.ndim == 2 else (a, chunked(a.shape)) for a in (*whole, *blocks)]
    out_specs = [chunked(s) if cut else resident(s) for s, _, cut in outs]
    out_shape = [jax.ShapeDtypeStruct(s, d) for s, d, _ in outs]
    moved = sum(a.size * a.dtype.itemsize for a, _ in order)
    moved += sum(s.size * s.dtype.itemsize for s in out_shape)
    return pl.pallas_call(
        kernel,
        out_shape=out_shape,
        grid_spec=pltpu.PrefetchScalarGridSpec(
            num_scalar_prefetch=1,
            grid=(steps,),
            in_specs=[s for _, s in order],
            out_specs=out_specs,
            scratch_shapes=[pltpu.VMEM(acc, F32)] if acc else [],
        ),
        compiler_params=pltpu.CompilerParams(vmem_limit_bytes=40 * 2**20),
        cost_estimate=pl.CostEstimate(flops=4 * flops, bytes_accessed=moved, transcendentals=0),
        name=name,
    )(ids, *[a for a, _ in order])


def per_device(
    history,
    depth_weights,
    depth_index,
    gain,
    gate_blocks,
    up_blocks,
    down_blocks,
    block_ids,
    grad_out,
):
    tokens, width = grad_out.shape
    owned, size = gate_blocks.shape[:2]
    tensor_count = lax.axis_size("tensor")
    dp_count = lax.axis_size("dp")
    chips = dp_count // 2
    hidden_width = FF // tensor_count
    share_width = width // tensor_count
    share_start = lax.axis_index("tensor") * share_width
    dp = lax.axis_index("dp")
    chip, core = dp // 2, dp % 2
    active = block_ids.shape[0]
    ids = block_ids.reshape(-1)
    flops = 2 * active * size * size * tokens

    gate_all = lax.all_gather(gate_blocks, "dp", axis=0, tiled=True)
    up_all = lax.all_gather(up_blocks, "dp", axis=0, tiled=True)
    down_all = lax.all_gather(down_blocks, "dp", axis=0, tiled=True)

    def share(a):
        return lax.dynamic_slice_in_dim(a, share_start, share_width, a.ndim - 1)

    mixed = jnp.zeros((tokens, width), F32)
    for slot in range(depth_index.shape[0]):
        earlier = lax.dynamic_index_in_dim(history, depth_index[slot], 0, keepdims=False)
        mixed = mixed + depth_weights[slot] * earlier.astype(F32)
    scale_inv = lax.rsqrt(jnp.mean(mixed * mixed, axis=-1, keepdims=True) + EPSILON)
    normed = (mixed * scale_inv * gain).astype(BF16)

    acts = (tokens, hidden_width)
    (gate_pre,) = call(gate_kernel, ids, [normed], [gate_all], [(acts, F32, False)], flops, CHUNKS, name="gate")
    up_pre, hidden = call(
        up_kernel, ids, [normed], [up_all, gate_pre], [(acts, F32, False), (acts, BF16, False)],
        flops, CHUNKS, name="up_hidden",
    )

    owner_ids = block_ids.reshape(chips, 2, owned, 2)

    def half_ids(which):
        return lax.dynamic_index_in_dim(owner_ids, which, 1, keepdims=False).reshape(-1)

    other_ids, own_ids = half_ids(1 - core), half_ids(core)
    half = (chips * owned, size, size)
    siblings = [(i, i ^ 1) for i in range(dp_count)]

    def down_grads(which):
        return call(
            down_grad_kernel, which, [hidden, grad_out], [], [(half, BF16, True)],
            flops // 2, chips, name="down_grad",
        )

    def line_sum(own, received):
        parts = own.astype(F32) + received.astype(F32)
        parts = parts.astype(BF16).reshape(chips, owned, size, size)
        from_below = from_above = None
        for step in range(chips - 1):
            reach = chips - 1 - step

            def piece(target, arrived):
                p = lax.dynamic_index_in_dim(parts, jnp.clip(target, 0, chips - 1), 0, keepdims=False)
                if arrived is None:
                    return p
                return (p.astype(F32) + arrived.astype(F32)).astype(BF16)

            upward = piece(chip + reach, from_below)
            downward = piece(chip - reach, from_above)
            pairs = [(z, z + 1) for z in range(min(step + 1, chips - 1))]
            up_pairs = [(2 * a + c, 2 * b + c) for a, b in pairs for c in (0, 1)]
            down_pairs = [
                (2 * (chips - 1 - a) + c, 2 * (chips - 1 - b) + c) for a, b in pairs for c in (0, 1)
            ]
            from_below = lax.ppermute(upward, "dp", up_pairs)
            from_above = lax.ppermute(downward, "dp", down_pairs)
        total = lax.dynamic_index_in_dim(parts, chip, 0, keepdims=False).astype(F32)
        if from_below is not None:
            total = total + from_below.astype(F32) + from_above.astype(F32)
        return total

    (down_other,) = down_grads(other_ids)
    down_received = lax.ppermute(down_other, "dp", siblings)
    (down_own,) = down_grads(own_ids)
    grad_down = line_sum(down_own, down_received)

    dgate, dup = call(
        hidden_grad_kernel, ids, [grad_out], [down_all, gate_pre, up_pre],
        [(acts, BF16, False), (acts, BF16, False)], flops, CHUNKS, acc=acts, name="hidden_grad",
    )

    def gate_up_grads(which):
        return call(
            gate_up_grad_kernel, which, [normed, dgate, dup], [], [(half, BF16, True), (half, BF16, True)],
            flops, chips, name="gate_up_grad",
        )

    gate_other, up_other = gate_up_grads(other_ids)
    gate_received = lax.ppermute(gate_other, "dp", siblings)
    up_received = lax.ppermute(up_other, "dp", siblings)
    gate_own, up_own = gate_up_grads(own_ids)
    grad_gate = line_sum(gate_own, gate_received)
    grad_up = line_sum(up_own, up_received)

    rows = (tokens, width)
    (ffn,) = call(
        ffn_kernel, ids, [hidden], [down_all], [(rows, BF16, False)], flops, CHUNKS, acc=rows, name="ffn"
    )
    (normed_grad,) = call(
        normed_grad_kernel, ids, [dgate, dup], [gate_all, up_all], [(rows, BF16, False)],
        2 * flops, CHUNKS, acc=rows, name="normed_grad",
    )
    ffn_share = lax.psum_scatter(ffn, "tensor", scatter_dimension=1, tiled=True).astype(F32)
    mixed_share = share(mixed)
    layer_out = (mixed_share + ffn_share).astype(BF16)

    grad_share = lax.psum_scatter(normed_grad, "tensor", scatter_dimension=1, tiled=True).astype(F32)
    gain_share = share(gain)
    along = lax.psum(jnp.sum(grad_share * gain_share * mixed_share, axis=-1, keepdims=True), "tensor")
    grad_mixed = (
        share(grad_out).astype(F32)
        + scale_inv * gain_share * grad_share
        - mixed_share * (scale_inv * scale_inv * scale_inv / width) * along
    )
    gain_part = jnp.sum(grad_share * mixed_share * scale_inv, axis=0)
    depth_list = []
    for slot in range(depth_index.shape[0]):
        earlier = lax.dynamic_index_in_dim(history, depth_index[slot], 0, keepdims=False)
        depth_list.append(jnp.sum(grad_mixed * share(earlier).astype(F32)))
    gain_sum = lax.psum(gain_part, "dp")
    depth_sum = lax.psum(jnp.stack(depth_list), ("dp", "tensor"))
    return (layer_out, grad_mixed, grad_gate, grad_up, grad_down, depth_sum, gain_sum)


def solution(mesh):
    placed = (
        P(None, "dp", None),
        P(),
        P(),
        P(),
        P(("tensor", "dp"), None, None),
        P(("tensor", "dp"), None, None),
        P(("tensor", "dp"), None, None),
        P("tensor", None),
        P("dp", None),
    )
    return jax.shard_map(
        per_device,
        mesh=mesh,
        in_specs=placed,
        out_specs=(
            P("dp", "tensor"),
            P("dp", "tensor"),
            P(("tensor", "dp"), None, None),
            P(("tensor", "dp"), None, None),
            P(("tensor", "dp"), None, None),
            P(),
            P("tensor"),
        ),
        check_vma=False,
    )
```

```python
import jax
import jax.numpy as jnp
from jax import lax
from jax.experimental import pallas as pl
from jax.experimental.pallas import tpu as pltpu
from jax.sharding import PartitionSpec as P

FF = 14336
EPSILON = 1e-05
CHUNKS = 8
UNROLL = 7
F32 = jnp.float32
BF16 = jnp.bfloat16
NN = (((1,), (0,)), ((), ()))
NT = (((1,), (1,)), ((), ()))
TN = (((0,), (0,)), ((), ()))


def dot(a, b, dims):
    return lax.dot_general(a, b, dims, preferred_element_type=F32)


def lanes(index, size):
    return pl.ds(pl.multiple_of(index * size, size), size)


def for_blocks(ids, first, count, body):
    def step(i, carry):
        for u in range(UNROLL):
            b = i * UNROLL + u
            body(b, ids[2 * (first + b)], ids[2 * (first + b) + 1])
        return carry

    lax.fori_loop(0, count // UNROLL, step, 0)


def for_columns(size, width, body):
    def step(c, carry):
        body(lanes(c, size))
        return carry

    lax.fori_loop(0, width // size, step, 0)


def gate_kernel(ids, x, w, acc):
    n, size = w.shape[0], w.shape[1]

    @pl.when(pl.program_id(0) == 0)
    def _():
        acc[...] = jnp.zeros_like(acc)

    def body(b, r, c):
        acc[:, lanes(c, size)] += dot(x[:, lanes(r, size)], w[b], NN)

    for_blocks(ids, pl.program_id(0) * n, n, body)


def up_kernel(ids, x, w, gate, acc, hidden):
    n, size = w.shape[0], w.shape[1]
    gate_kernel(ids, x, w, acc)

    @pl.when(pl.program_id(0) == pl.num_programs(0) - 1)
    def _():
        def body(cols):
            g = gate[:, cols]
            hidden[:, cols] = (g / (1.0 + jnp.exp(-g)) * acc[:, cols]).astype(BF16)

        for_columns(size, acc.shape[1], body)


def hidden_grad_kernel(ids, gout, w, gate, up, dgate, dup, acc):
    n, size = w.shape[0], w.shape[1]

    @pl.when(pl.program_id(0) == 0)
    def _():
        acc[...] = jnp.zeros_like(acc)

    def body(b, r, c):
        acc[:, lanes(c, size)] += dot(gout[:, lanes(r, size)], w[b], NT)

    for_blocks(ids, pl.program_id(0) * n, n, body)

    @pl.when(pl.program_id(0) == pl.num_programs(0) - 1)
    def _():
        def finish(cols):
            g = gate[:, cols]
            s = 1.0 / (1.0 + jnp.exp(-g))
            gh = acc[:, cols]
            dgate[:, cols] = (gh * up[:, cols] * s * (1.0 + g * (1.0 - s))).astype(BF16)
            dup[:, cols] = (gh * g * s).astype(BF16)

        for_columns(size, acc.shape[1], finish)


def ffn_kernel(ids, hidden, w, out, acc):
    n, size = w.shape[0], w.shape[1]

    @pl.when(pl.program_id(0) == 0)
    def _():
        acc[...] = jnp.zeros_like(acc)

    def body(b, r, c):
        acc[:, lanes(r, size)] += dot(hidden[:, lanes(c, size)], w[b], NN)

    for_blocks(ids, pl.program_id(0) * n, n, body)

    @pl.when(pl.program_id(0) == pl.num_programs(0) - 1)
    def _():
        out[...] = acc[...].astype(BF16)


def normed_grad_kernel(ids, dgate, dup, gate_w, up_w, out, acc):
    n, size = gate_w.shape[0], gate_w.shape[1]

    @pl.when(pl.program_id(0) == 0)
    def _():
        acc[...] = jnp.zeros_like(acc)

    def body(b, r, c):
        left = jnp.concatenate([dgate[:, lanes(c, size)], dup[:, lanes(c, size)]], axis=1)
        right = jnp.concatenate([gate_w[b], up_w[b]], axis=1)
        acc[:, lanes(r, size)] += dot(left, right, NT)

    for_blocks(ids, pl.program_id(0) * n, n, body)

    @pl.when(pl.program_id(0) == pl.num_programs(0) - 1)
    def _():
        out[...] = acc[...].astype(BF16)


def down_grad_kernel(ids, hidden, gout, out):
    n, size = out.shape[0], out.shape[1]

    def body(b, r, c):
        out[b] = dot(hidden[:, lanes(c, size)], gout[:, lanes(r, size)], TN).astype(BF16)

    for_blocks(ids, pl.program_id(0) * n, n, body)


def gate_up_grad_kernel(ids, x, dgate, dup, out_gate, out_up):
    n, size = out_gate.shape[0], out_gate.shape[1]

    def body(b, r, c):
        right = jnp.concatenate([dgate[:, lanes(c, size)], dup[:, lanes(c, size)]], axis=1)
        both = dot(x[:, lanes(r, size)], right, TN).astype(BF16)
        out_gate[b] = both[:, :size]
        out_up[b] = both[:, size:]

    for_blocks(ids, pl.program_id(0) * n, n, body)


def call(kernel, ids, whole, blocks, outs, flops, steps, acc=None, name=None, after=()):
    read = 1 + len(whole) + len(blocks)

    def body(*refs):
        kernel(*refs[:read], *refs[read + len(after) :])

    chunked = lambda shape: pl.BlockSpec((shape[0] // steps, *shape[1:]), lambda i, ids: (i, 0, 0))
    resident = lambda shape: pl.BlockSpec(shape, lambda i, ids: (0, 0))
    order = [(a, resident(a.shape)) if a.ndim == 2 else (a, chunked(a.shape)) for a in (*whole, *blocks)]
    out_specs = [chunked(s) if cut else resident(s) for s, _, cut in outs]
    out_shape = [jax.ShapeDtypeStruct(s, d) for s, d, _ in outs]
    moved = sum(a.size * a.dtype.itemsize for a, _ in order)
    moved += sum(s.size * s.dtype.itemsize for s in out_shape)
    return pl.pallas_call(
        body,
        out_shape=out_shape,
        grid_spec=pltpu.PrefetchScalarGridSpec(
            num_scalar_prefetch=1,
            grid=(steps,),
            in_specs=[s for _, s in order] + [pl.BlockSpec(memory_space=pl.ANY)] * len(after),
            out_specs=out_specs,
            scratch_shapes=[pltpu.VMEM(acc, F32)] if acc else [],
        ),
        compiler_params=pltpu.CompilerParams(vmem_limit_bytes=40 * 2**20),
        cost_estimate=pl.CostEstimate(flops=4 * flops, bytes_accessed=moved, transcendentals=0),
        name=name,
    )(ids, *[a for a, _ in order], *after)


def per_device(
    history,
    depth_weights,
    depth_index,
    gain,
    gate_blocks,
    up_blocks,
    down_blocks,
    block_ids,
    grad_out,
):
    tokens, width = grad_out.shape
    owned, size = gate_blocks.shape[:2]
    tensor_count = lax.axis_size("tensor")
    dp_count = lax.axis_size("dp")
    chips = dp_count // 2
    hidden_width = FF // tensor_count
    share_width = width // tensor_count
    share_start = lax.axis_index("tensor") * share_width
    dp = lax.axis_index("dp")
    chip, core = dp // 2, dp % 2
    active = block_ids.shape[0]
    ids = block_ids.reshape(-1)
    flops = 2 * active * size * size * tokens

    gate_all = lax.all_gather(gate_blocks, "dp", axis=0, tiled=True)
    up_all = lax.all_gather(up_blocks, "dp", axis=0, tiled=True)
    down_all = lax.all_gather(down_blocks, "dp", axis=0, tiled=True)

    def share(a):
        return lax.dynamic_slice_in_dim(a, share_start, share_width, a.ndim - 1)

    mixed = jnp.zeros((tokens, width), F32)
    for slot in range(depth_index.shape[0]):
        earlier = lax.dynamic_index_in_dim(history, depth_index[slot], 0, keepdims=False)
        mixed = mixed + depth_weights[slot] * earlier.astype(F32)
    scale_inv = lax.rsqrt(jnp.mean(mixed * mixed, axis=-1, keepdims=True) + EPSILON)
    normed = (mixed * scale_inv * gain).astype(BF16)

    acts = (tokens, hidden_width)
    (gate_pre,) = call(gate_kernel, ids, [normed], [gate_all], [(acts, F32, False)], flops, CHUNKS, name="gate")
    up_pre, hidden = call(
        up_kernel, ids, [normed], [up_all, gate_pre], [(acts, F32, False), (acts, BF16, False)],
        flops, CHUNKS, name="up_hidden",
    )

    owner_ids = block_ids.reshape(chips, 2, owned, 2)

    def half_ids(which):
        return lax.dynamic_index_in_dim(owner_ids, which, 1, keepdims=False).reshape(-1)

    other_ids, own_ids = half_ids(1 - core), half_ids(core)
    half = (chips * owned, size, size)
    siblings = [(i, i ^ 1) for i in range(dp_count)]

    def down_grads(which, after=()):
        return call(
            down_grad_kernel, which, [hidden, grad_out], [], [(half, BF16, True)],
            flops // 2, chips, name="down_grad", after=after,
        )

    def line_sum(own, received):
        own = own.reshape(chips, owned, size, size)
        received = received.reshape(chips, owned, size, size)

        def part(target):
            target = jnp.clip(target, 0, chips - 1)
            a = lax.dynamic_index_in_dim(own, target, 0, keepdims=False)
            b = lax.dynamic_index_in_dim(received, target, 0, keepdims=False)
            return a.astype(F32) + b.astype(F32)

        from_below = from_above = None
        for step in range(chips - 1):
            reach = chips - 1 - step
            upward, downward = part(chip + reach), part(chip - reach)
            if step:
                upward = upward + from_below.astype(F32)
                downward = downward + from_above.astype(F32)
            upward, downward = upward.astype(BF16), downward.astype(BF16)
            pairs = [(z, z + 1) for z in range(step + 1)]
            up_pairs = [(2 * a + c, 2 * b + c) for a, b in pairs for c in (0, 1)]
            down_pairs = [
                (2 * (chips - 1 - a) + c, 2 * (chips - 1 - b) + c) for a, b in pairs for c in (0, 1)
            ]
            from_below = lax.ppermute(upward, "dp", up_pairs)
            from_above = lax.ppermute(downward, "dp", down_pairs)
            yield [upward, downward]
        total = part(chip)
        if from_below is not None:
            total = total + from_below.astype(F32) + from_above.astype(F32)
        yield total

    (down_other,) = down_grads(other_ids)
    down_received = lax.ppermute(down_other, "dp", siblings)
    (down_own,) = down_grads(own_ids, [down_other])
    down_line = list(line_sum(down_own, down_received))
    grad_down = down_line[-1]

    dgate, dup = call(
        hidden_grad_kernel, ids, [grad_out], [down_all, gate_pre, up_pre],
        [(acts, BF16, False), (acts, BF16, False)], flops, CHUNKS, acc=acts, name="hidden_grad",
        after=down_line[min(1, chips - 2)] if chips > 1 else (),
    )

    def gate_up_grads(which, after=()):
        return call(
            gate_up_grad_kernel, which, [normed, dgate, dup], [], [(half, BF16, True), (half, BF16, True)],
            flops, chips, name="gate_up_grad", after=after,
        )

    gate_other, up_other = gate_up_grads(other_ids, down_line[-2] if chips > 1 else ())
    gate_received = lax.ppermute(gate_other, "dp", siblings)
    up_received = lax.ppermute(up_other, "dp", siblings)
    gate_own, up_own = gate_up_grads(own_ids, [gate_other])
    gate_line = list(line_sum(gate_own, gate_received))
    up_line = list(line_sum(up_own, up_received))
    grad_gate, grad_up = gate_line[-1], up_line[-1]
    first = (gate_line[0] + up_line[0]) if chips > 1 else []
    last = (gate_line[-2] + up_line[-2]) if chips > 1 else []

    rows = (tokens, width)
    (normed_grad,) = call(
        normed_grad_kernel, ids, [dgate, dup], [gate_all, up_all], [(rows, BF16, False)],
        2 * flops, CHUNKS, acc=rows, name="normed_grad", after=first,
    )
    (ffn,) = call(
        ffn_kernel, ids, [hidden], [down_all], [(rows, BF16, False)], flops, CHUNKS, acc=rows, name="ffn",
        after=[normed_grad],
    )
    grad_share = lax.psum_scatter(normed_grad, "tensor", scatter_dimension=1, tiled=True).astype(F32)
    ffn_share = lax.psum_scatter(ffn, "tensor", scatter_dimension=1, tiled=True).astype(F32)
    mixed_share = share(mixed)
    layer_out = (mixed_share + ffn_share).astype(BF16)

    gain_share = share(gain)
    cubed = scale_inv * scale_inv * scale_inv / width
    direct = share(grad_out).astype(F32) + scale_inv * gain_share * grad_share
    along_part = jnp.sum(grad_share * gain_share * mixed_share, axis=-1)
    gain_part = jnp.sum(grad_share * mixed_share * scale_inv, axis=0)
    depth_list = []
    for slot in range(depth_index.shape[0]):
        earlier = lax.dynamic_index_in_dim(history, depth_index[slot], 0, keepdims=False).astype(F32)
        second = jnp.sum(mixed * earlier, axis=-1) * cubed[:, 0]
        depth_list.append(jnp.sum(direct * share(earlier)) - jnp.sum(along_part * second))
    slots = depth_index.shape[0]
    sums = jnp.zeros((slots + width + dp_count * tokens,), F32)
    sums = lax.dynamic_update_slice_in_dim(sums, jnp.stack(depth_list), 0, 0)
    sums = lax.dynamic_update_slice_in_dim(sums, gain_part, slots + share_start, 0)
    sums = lax.dynamic_update_slice_in_dim(sums, along_part, slots + width + dp * tokens, 0)
    sums = lax.optimization_barrier((sums, *last))[0]
    sums = lax.psum(sums, ("dp", "tensor"))
    depth_sum = sums[:slots]
    gain_sum = lax.dynamic_slice_in_dim(sums, slots + share_start, share_width, 0)
    along = lax.dynamic_slice_in_dim(sums, slots + width + dp * tokens, tokens, 0)[:, None]
    grad_mixed = direct - mixed_share * cubed * along
    return (layer_out, grad_mixed, grad_gate, grad_up, grad_down, depth_sum, gain_sum)


def solution(mesh):
    placed = (
        P(None, "dp", None),
        P(),
        P(),
        P(),
        P(("tensor", "dp"), None, None),
        P(("tensor", "dp"), None, None),
        P(("tensor", "dp"), None, None),
        P("tensor", None),
        P("dp", None),
    )
    return jax.shard_map(
        per_device,
        mesh=mesh,
        in_specs=placed,
        out_specs=(
            P("dp", "tensor"),
            P("dp", "tensor"),
            P(("tensor", "dp"), None, None),
            P(("tensor", "dp"), None, None),
            P(("tensor", "dp"), None, None),
            P(),
            P("tensor"),
        ),
        check_vma=False,
    )
```

```python
import jax
import jax.numpy as jnp
from jax import lax
from jax.experimental import pallas as pl
from jax.experimental.pallas import tpu as pltpu
from jax.sharding import PartitionSpec as P

FF = 14336
EPSILON = 1e-05
CHUNKS = 8
UNROLL = 7
F32 = jnp.float32
BF16 = jnp.bfloat16
NN = (((1,), (0,)), ((), ()))
NT = (((1,), (1,)), ((), ()))
TN = (((0,), (0,)), ((), ()))


def dot(a, b, dims):
    return lax.dot_general(a, b, dims, preferred_element_type=F32)


def lanes(index, size):
    return pl.ds(pl.multiple_of(index * size, size), size)


def for_blocks(ids, first, count, body):
    def step(i, carry):
        for u in range(UNROLL):
            b = i * UNROLL + u
            body(b, ids[2 * (first + b)], ids[2 * (first + b) + 1])
        return carry

    lax.fori_loop(0, count // UNROLL, step, 0)


def for_columns(size, width, body):
    def step(c, carry):
        body(lanes(c, size))
        return carry

    lax.fori_loop(0, width // size, step, 0)


def gate_kernel(ids, x, w, acc):
    n, size = w.shape[0], w.shape[1]

    @pl.when(pl.program_id(0) == 0)
    def _():
        acc[...] = jnp.zeros_like(acc)

    def body(b, r, c):
        acc[:, lanes(c, size)] += dot(x[:, lanes(r, size)], w[b], NN)

    for_blocks(ids, pl.program_id(0) * n, n, body)


def up_kernel(ids, x, w, gate, acc, hidden):
    n, size = w.shape[0], w.shape[1]
    gate_kernel(ids, x, w, acc)

    @pl.when(pl.program_id(0) == pl.num_programs(0) - 1)
    def _():
        def body(cols):
            g = gate[:, cols]
            hidden[:, cols] = (g / (1.0 + jnp.exp(-g)) * acc[:, cols]).astype(BF16)

        for_columns(size, acc.shape[1], body)


def hidden_grad_kernel(ids, gout, w, gate, up, dgate, dup, acc):
    n, size = w.shape[0], w.shape[1]

    @pl.when(pl.program_id(0) == 0)
    def _():
        acc[...] = jnp.zeros_like(acc)

    def body(b, r, c):
        acc[:, lanes(c, size)] += dot(gout[:, lanes(r, size)], w[b], NT)

    for_blocks(ids, pl.program_id(0) * n, n, body)

    @pl.when(pl.program_id(0) == pl.num_programs(0) - 1)
    def _():
        def finish(cols):
            g = gate[:, cols]
            s = 1.0 / (1.0 + jnp.exp(-g))
            gh = acc[:, cols]
            dgate[:, cols] = (gh * up[:, cols] * s * (1.0 + g * (1.0 - s))).astype(BF16)
            dup[:, cols] = (gh * g * s).astype(BF16)

        for_columns(size, acc.shape[1], finish)


def ffn_kernel(ids, hidden, w, out, acc):
    n, size = w.shape[0], w.shape[1]

    @pl.when(pl.program_id(0) == 0)
    def _():
        acc[...] = jnp.zeros_like(acc)

    def body(b, r, c):
        acc[:, lanes(r, size)] += dot(hidden[:, lanes(c, size)], w[b], NN)

    for_blocks(ids, pl.program_id(0) * n, n, body)

    @pl.when(pl.program_id(0) == pl.num_programs(0) - 1)
    def _():
        out[...] = acc[...].astype(BF16)


def normed_grad_kernel(ids, dgate, dup, gate_w, up_w, out, acc):
    n, size = gate_w.shape[0], gate_w.shape[1]

    @pl.when(pl.program_id(0) == 0)
    def _():
        acc[...] = jnp.zeros_like(acc)

    def body(b, r, c):
        left = jnp.concatenate([dgate[:, lanes(c, size)], dup[:, lanes(c, size)]], axis=1)
        right = jnp.concatenate([gate_w[b], up_w[b]], axis=1)
        acc[:, lanes(r, size)] += dot(left, right, NT)

    for_blocks(ids, pl.program_id(0) * n, n, body)

    @pl.when(pl.program_id(0) == pl.num_programs(0) - 1)
    def _():
        out[...] = acc[...].astype(BF16)


def down_grad_kernel(ids, hidden, gout, out):
    n, size = out.shape[2], out.shape[3]

    def body(b, r, c):
        out[0, 0, b] = dot(hidden[:, lanes(c, size)], gout[:, lanes(r, size)], TN).astype(BF16)

    for_blocks(ids, pl.program_id(0) * n, n, body)


def gate_up_grad_kernel(ids, x, dgate, dup, out):
    n, size = out.shape[2], out.shape[3]

    def body(b, r, c):
        right = jnp.concatenate([dgate[:, lanes(c, size)], dup[:, lanes(c, size)]], axis=1)
        both = dot(x[:, lanes(r, size)], right, TN).astype(BF16)
        out[0, 0, b] = both[:, :size]
        out[0, 1, b] = both[:, size:]

    for_blocks(ids, pl.program_id(0) * n, n, body)


def line_sum_kernel(own, other, out, held, below, above, pair_send, pair_recv, up_send, up_recv, down_send, down_recv):
    chips, arrays, owned = own.shape[:3]
    dp = lax.axis_index("dp")
    tensor = lax.axis_index("tensor")
    chip, core = dp // 2, dp % 2
    sibling = (chip * 2 + 1 - core, tensor)
    upper, lower = (dp + 2, tensor), (dp - 2, tensor)
    has_upper, has_lower = chip < chips - 1, chip > 0
    mesh_id = pl.DeviceIdType.MESH

    barrier = pltpu.get_barrier_semaphore()
    pl.semaphore_signal(barrier, inc=1, device_id=sibling, device_id_type=mesh_id)

    @pl.when(has_upper)
    def _():
        pl.semaphore_signal(barrier, inc=1, device_id=upper, device_id_type=mesh_id)

    @pl.when(has_lower)
    def _():
        pl.semaphore_signal(barrier, inc=1, device_id=lower, device_id_type=mesh_id)

    pl.semaphore_wait(barrier, 1 + has_upper.astype(jnp.int32) + has_lower.astype(jnp.int32))

    def pair_copy(j, a):
        return pltpu.make_async_remote_copy(
            src_ref=other.at[j, a], dst_ref=held.at[j, a],
            send_sem=pair_send.at[j, a], recv_sem=pair_recv.at[j, a],
            device_id=sibling, device_id_type=mesh_id,
        )

    def up_copy(step, a):
        return pltpu.make_async_remote_copy(
            src_ref=held.at[lax.rem(chips - 1 - step + chip, chips), a], dst_ref=below.at[step, a],
            send_sem=up_send.at[step, a], recv_sem=up_recv.at[step, a],
            device_id=upper, device_id_type=mesh_id,
        )

    def down_copy(step, a):
        return pltpu.make_async_remote_copy(
            src_ref=held.at[lax.rem(chip + 1 + step, chips), a], dst_ref=above.at[step, a],
            send_sem=down_send.at[step, a], recv_sem=down_recv.at[step, a],
            device_id=lower, device_id_type=mesh_id,
        )

    for k in range(chips):
        j = jnp.where(2 * chip < chips, chips - 1 - k, k)
        for a in range(arrays):
            pair_copy(j, a).start()

    def add(j, a, arrived):
        def body(b, carry):
            total = own[j, a, b].astype(F32) + held[j, a, b].astype(F32)
            if arrived is not None:
                total = total + arrived[b].astype(F32)
            held[j, a, b] = total.astype(BF16)
            return carry

        lax.fori_loop(0, owned, body, 0)

    def pass_on(step, a, sends, first, j, copy, arrived):
        @pl.when(sends)
        def _():
            pair_copy(j, a).wait_recv()

            @pl.when(first)
            def _():
                add(j, a, None)

            if step:

                @pl.when(jnp.logical_not(first))
                def _():
                    copy(step - 1, a).wait_recv()
                    add(j, a, arrived.at[step - 1, a])

                @pl.when(sends_at(step - 1, first, chip, copy))
                def _():
                    copy(step - 1, a).wait_send()

            copy(step, a).start()

    def sends_at(step, first, chip, copy):
        return chip <= step if copy is up_copy else chips - 1 - chip <= step

    for step in range(chips - 1):
        for a in range(arrays):
            pass_on(
                step, a, jnp.logical_and(has_upper, chip <= step), chip == 0,
                lax.rem(chips - 1 - step + chip, chips), up_copy, below,
            )
            pass_on(
                step, a, jnp.logical_and(has_lower, chips - 1 - chip <= step), chip == chips - 1,
                lax.rem(chip + 1 + step, chips), down_copy, above,
            )

    for a in range(arrays):
        pair_copy(chip, a).wait_recv()

        @pl.when(has_lower)
        def _():
            up_copy(chips - 2, a).wait_recv()

        @pl.when(has_upper)
        def _():
            down_copy(chips - 2, a).wait_recv()

        def base(b):
            return own[chip, a, b].astype(F32) + held[chip, a, b].astype(F32)

        def each(value):
            def body(b, carry):
                out[a, b] = value(b)
                return carry

            lax.fori_loop(0, owned, body, 0)

        inner = jnp.logical_and(has_lower, has_upper)

        @pl.when(inner)
        def _():
            each(lambda b: base(b) + below[chips - 2, a, b].astype(F32) + above[chips - 2, a, b].astype(F32))

        @pl.when(jnp.logical_and(has_lower, jnp.logical_not(has_upper)))
        def _():
            each(lambda b: base(b) + below[chips - 2, a, b].astype(F32))

        @pl.when(jnp.logical_and(has_upper, jnp.logical_not(has_lower)))
        def _():
            each(lambda b: base(b) + above[chips - 2, a, b].astype(F32))

        for j in range(chips):
            pair_copy(j, a).wait_send()

        @pl.when(has_upper)
        def _():
            up_copy(chips - 2, a).wait_send()

        @pl.when(has_lower)
        def _():
            down_copy(chips - 2, a).wait_send()


def line_sum(own, other, collective_id, name):
    chips, arrays = own.shape[:2]
    piece = own.shape[2:]
    line = (chips - 1, arrays)
    return pl.pallas_call(
        line_sum_kernel,
        out_shape=jax.ShapeDtypeStruct(own.shape[1:], F32),
        in_specs=[pl.BlockSpec(memory_space=pltpu.VMEM)] * 2,
        out_specs=pl.BlockSpec(memory_space=pltpu.VMEM),
        scratch_shapes=[
            pltpu.VMEM(own.shape, BF16),
            pltpu.VMEM((*line, *piece), BF16),
            pltpu.VMEM((*line, *piece), BF16),
            pltpu.SemaphoreType.DMA((chips, arrays)),
            pltpu.SemaphoreType.DMA((chips, arrays)),
            pltpu.SemaphoreType.DMA(line),
            pltpu.SemaphoreType.DMA(line),
            pltpu.SemaphoreType.DMA(line),
            pltpu.SemaphoreType.DMA(line),
        ],
        compiler_params=pltpu.CompilerParams(
            collective_id=collective_id, has_side_effects=True, vmem_limit_bytes=56 * 2**20
        ),
        cost_estimate=pl.CostEstimate(
            flops=own.size, bytes_accessed=64 * own.size, transcendentals=0
        ),
        name=name,
    )(own, other)


def call(kernel, ids, whole, blocks, outs, flops, steps, acc=None, name=None, after=()):
    read = 1 + len(whole) + len(blocks)

    def body(*refs):
        kernel(*refs[:read], *refs[read + len(after) :])

    chunked = lambda shape: pl.BlockSpec(
        (shape[0] // steps, *shape[1:]), lambda i, ids: (i, *[0] * (len(shape) - 1))
    )
    resident = lambda shape: pl.BlockSpec(shape, lambda i, ids: (0, 0))
    order = [(a, resident(a.shape)) if a.ndim == 2 else (a, chunked(a.shape)) for a in (*whole, *blocks)]
    out_specs = [chunked(s) if cut else resident(s) for s, _, cut in outs]
    out_shape = [jax.ShapeDtypeStruct(s, d) for s, d, _ in outs]
    moved = sum(a.size * a.dtype.itemsize for a, _ in order)
    moved += sum(s.size * s.dtype.itemsize for s in out_shape)
    return pl.pallas_call(
        body,
        out_shape=out_shape,
        grid_spec=pltpu.PrefetchScalarGridSpec(
            num_scalar_prefetch=1,
            grid=(steps,),
            in_specs=[s for _, s in order] + [pl.BlockSpec(memory_space=pl.ANY)] * len(after),
            out_specs=out_specs,
            scratch_shapes=[pltpu.VMEM(acc, F32)] if acc else [],
        ),
        compiler_params=pltpu.CompilerParams(vmem_limit_bytes=40 * 2**20),
        cost_estimate=pl.CostEstimate(flops=4 * flops, bytes_accessed=moved, transcendentals=0),
        name=name,
    )(ids, *[a for a, _ in order], *after)


def per_device(
    history,
    depth_weights,
    depth_index,
    gain,
    gate_blocks,
    up_blocks,
    down_blocks,
    block_ids,
    grad_out,
):
    tokens, width = grad_out.shape
    owned, size = gate_blocks.shape[:2]
    tensor_count = lax.axis_size("tensor")
    dp_count = lax.axis_size("dp")
    chips = dp_count // 2
    hidden_width = FF // tensor_count
    share_width = width // tensor_count
    share_start = lax.axis_index("tensor") * share_width
    dp = lax.axis_index("dp")
    chip, core = dp // 2, dp % 2
    active = block_ids.shape[0]
    ids = block_ids.reshape(-1)
    flops = 2 * active * size * size * tokens

    gate_all = lax.all_gather(gate_blocks, "dp", axis=0, tiled=True)
    up_all = lax.all_gather(up_blocks, "dp", axis=0, tiled=True)
    down_all = lax.all_gather(down_blocks, "dp", axis=0, tiled=True)

    def share(a):
        return lax.dynamic_slice_in_dim(a, share_start, share_width, a.ndim - 1)

    mixed = jnp.zeros((tokens, width), F32)
    for slot in range(depth_index.shape[0]):
        earlier = lax.dynamic_index_in_dim(history, depth_index[slot], 0, keepdims=False)
        mixed = mixed + depth_weights[slot] * earlier.astype(F32)
    scale_inv = lax.rsqrt(jnp.mean(mixed * mixed, axis=-1, keepdims=True) + EPSILON)
    normed = (mixed * scale_inv * gain).astype(BF16)

    acts = (tokens, hidden_width)
    (gate_pre,) = call(gate_kernel, ids, [normed], [gate_all], [(acts, F32, False)], flops, CHUNKS, name="gate")
    up_pre, hidden = call(
        up_kernel, ids, [normed], [up_all, gate_pre], [(acts, F32, False), (acts, BF16, False)],
        flops, CHUNKS, name="up_hidden",
    )

    owner_ids = block_ids.reshape(chips, 2, owned, 2)

    def half_ids(which):
        return lax.dynamic_index_in_dim(owner_ids, which, 1, keepdims=False).reshape(-1)

    other_ids, own_ids = half_ids(1 - core), half_ids(core)

    def down_grads(which):
        (out,) = call(
            down_grad_kernel, which, [hidden, grad_out], [], [((chips, 1, owned, size, size), BF16, True)],
            flops // 2, chips, name="down_grad",
        )
        return out

    (grad_down,) = line_sum(down_grads(own_ids), down_grads(other_ids), 0, "down_line")

    dgate, dup = call(
        hidden_grad_kernel, ids, [grad_out], [down_all, gate_pre, up_pre],
        [(acts, BF16, False), (acts, BF16, False)], flops, CHUNKS, acc=acts, name="hidden_grad",
        after=[grad_down],
    )
    rows = (tokens, width)
    (normed_grad,) = call(
        normed_grad_kernel, ids, [dgate, dup], [gate_all, up_all], [(rows, BF16, False)],
        2 * flops, CHUNKS, acc=rows, name="normed_grad",
    )
    (ffn,) = call(
        ffn_kernel, ids, [hidden], [down_all], [(rows, BF16, False)], flops, CHUNKS, acc=rows, name="ffn",
        after=[normed_grad],
    )

    def gate_up_grads(which):
        (out,) = call(
            gate_up_grad_kernel, which, [normed, dgate, dup], [],
            [((chips, 2, owned, size, size), BF16, True)],
            flops, chips, name="gate_up_grad", after=[ffn],
        )
        return out

    grad_gate, grad_up = line_sum(gate_up_grads(own_ids), gate_up_grads(other_ids), 1, "gate_up_line")

    grad_share = lax.psum_scatter(normed_grad, "tensor", scatter_dimension=1, tiled=True).astype(F32)
    ffn_share = lax.psum_scatter(ffn, "tensor", scatter_dimension=1, tiled=True).astype(F32)
    mixed_share = share(mixed)
    layer_out = (mixed_share + ffn_share).astype(BF16)

    gain_share = share(gain)
    cubed = scale_inv * scale_inv * scale_inv / width
    direct = share(grad_out).astype(F32) + scale_inv * gain_share * grad_share
    along_part = jnp.sum(grad_share * gain_share * mixed_share, axis=-1)
    gain_part = jnp.sum(grad_share * mixed_share * scale_inv, axis=0)
    depth_list = []
    for slot in range(depth_index.shape[0]):
        earlier = lax.dynamic_index_in_dim(history, depth_index[slot], 0, keepdims=False).astype(F32)
        second = jnp.sum(mixed * earlier, axis=-1) * cubed[:, 0]
        depth_list.append(jnp.sum(direct * share(earlier)) - jnp.sum(along_part * second))
    slots = depth_index.shape[0]
    sums = jnp.zeros((slots + width + dp_count * tokens,), F32)
    sums = lax.dynamic_update_slice_in_dim(sums, jnp.stack(depth_list), 0, 0)
    sums = lax.dynamic_update_slice_in_dim(sums, gain_part, slots + share_start, 0)
    sums = lax.dynamic_update_slice_in_dim(sums, along_part, slots + width + dp * tokens, 0)
    sums = lax.optimization_barrier((sums, grad_gate))[0]
    sums = lax.psum(sums, ("dp", "tensor"))
    depth_sum = sums[:slots]
    gain_sum = lax.dynamic_slice_in_dim(sums, slots + share_start, share_width, 0)
    along = lax.dynamic_slice_in_dim(sums, slots + width + dp * tokens, tokens, 0)[:, None]
    grad_mixed = direct - mixed_share * cubed * along
    return (layer_out, grad_mixed, grad_gate, grad_up, grad_down, depth_sum, gain_sum)


def solution(mesh):
    placed = (
        P(None, "dp", None),
        P(),
        P(),
        P(),
        P(("tensor", "dp"), None, None),
        P(("tensor", "dp"), None, None),
        P(("tensor", "dp"), None, None),
        P("tensor", None),
        P("dp", None),
    )
    return jax.shard_map(
        per_device,
        mesh=mesh,
        in_specs=placed,
        out_specs=(
            P("dp", "tensor"),
            P("dp", "tensor"),
            P(("tensor", "dp"), None, None),
            P(("tensor", "dp"), None, None),
            P(("tensor", "dp"), None, None),
            P(),
            P("tensor"),
        ),
        check_vma=False,
    )
```

```python
import jax
import jax.numpy as jnp
from jax import lax
from jax.experimental import pallas as pl
from jax.experimental.pallas import tpu as pltpu
from jax.sharding import PartitionSpec as P

FF = 14336
EPSILON = 1e-05
CHUNKS = 8
UNROLL = 7
F32 = jnp.float32
BF16 = jnp.bfloat16
NN = (((1,), (0,)), ((), ()))
NT = (((1,), (1,)), ((), ()))
TN = (((0,), (0,)), ((), ()))


def dot(a, b, dims):
    return lax.dot_general(a, b, dims, preferred_element_type=F32)


def lanes(index, size):
    return pl.ds(pl.multiple_of(index * size, size), size)


def for_blocks(ids, first, count, body):
    def step(i, carry):
        for u in range(UNROLL):
            b = i * UNROLL + u
            body(b, ids[2 * (first + b)], ids[2 * (first + b) + 1])
        return carry

    lax.fori_loop(0, count // UNROLL, step, 0)


def for_columns(size, width, body):
    def step(c, carry):
        body(lanes(c, size))
        return carry

    lax.fori_loop(0, width // size, step, 0)


def gate_kernel(ids, x, w, acc):
    n, size = w.shape[0], w.shape[1]

    @pl.when(pl.program_id(0) == 0)
    def _():
        acc[...] = jnp.zeros_like(acc)

    def body(b, r, c):
        acc[:, lanes(c, size)] += dot(x[:, lanes(r, size)], w[b], NN)

    for_blocks(ids, pl.program_id(0) * n, n, body)


def up_kernel(ids, x, w, gate, acc, hidden):
    n, size = w.shape[0], w.shape[1]
    gate_kernel(ids, x, w, acc)

    @pl.when(pl.program_id(0) == pl.num_programs(0) - 1)
    def _():
        def body(cols):
            g = gate[:, cols]
            hidden[:, cols] = (g / (1.0 + jnp.exp(-g)) * acc[:, cols]).astype(BF16)

        for_columns(size, acc.shape[1], body)


def hidden_grad_kernel(ids, gout, w, gate, up, dgate, dup, acc):
    n, size = w.shape[0], w.shape[1]

    @pl.when(pl.program_id(0) == 0)
    def _():
        acc[...] = jnp.zeros_like(acc)

    def body(b, r, c):
        acc[:, lanes(c, size)] += dot(gout[:, lanes(r, size)], w[b], NT)

    for_blocks(ids, pl.program_id(0) * n, n, body)

    @pl.when(pl.program_id(0) == pl.num_programs(0) - 1)
    def _():
        def finish(cols):
            g = gate[:, cols]
            s = 1.0 / (1.0 + jnp.exp(-g))
            gh = acc[:, cols]
            dgate[:, cols] = (gh * up[:, cols] * s * (1.0 + g * (1.0 - s))).astype(BF16)
            dup[:, cols] = (gh * g * s).astype(BF16)

        for_columns(size, acc.shape[1], finish)


def ffn_kernel(ids, hidden, w, out, acc):
    n, size = w.shape[0], w.shape[1]

    @pl.when(pl.program_id(0) == 0)
    def _():
        acc[...] = jnp.zeros_like(acc)

    def body(b, r, c):
        acc[:, lanes(r, size)] += dot(hidden[:, lanes(c, size)], w[b], NN)

    for_blocks(ids, pl.program_id(0) * n, n, body)

    @pl.when(pl.program_id(0) == pl.num_programs(0) - 1)
    def _():
        out[...] = acc[...].astype(BF16)


def normed_grad_kernel(ids, dgate, dup, gate_w, up_w, out, acc):
    n, size = gate_w.shape[0], gate_w.shape[1]

    @pl.when(pl.program_id(0) == 0)
    def _():
        acc[...] = jnp.zeros_like(acc)

    def body(b, r, c):
        left = jnp.concatenate([dgate[:, lanes(c, size)], dup[:, lanes(c, size)]], axis=1)
        right = jnp.concatenate([gate_w[b], up_w[b]], axis=1)
        acc[:, lanes(r, size)] += dot(left, right, NT)

    for_blocks(ids, pl.program_id(0) * n, n, body)

    @pl.when(pl.program_id(0) == pl.num_programs(0) - 1)
    def _():
        out[...] = acc[...].astype(BF16)


def down_grad_kernel(ids, hidden, gout, out):
    n, size = out.shape[2], out.shape[3]

    def body(b, r, c):
        out[0, 0, b] = dot(hidden[:, lanes(c, size)], gout[:, lanes(r, size)], TN).astype(BF16)

    for_blocks(ids, pl.program_id(0) * n, n, body)


def gate_up_grad_kernel(ids, x, dgate, dup, out):
    n, size = out.shape[2], out.shape[3]

    def body(b, r, c):
        right = jnp.concatenate([dgate[:, lanes(c, size)], dup[:, lanes(c, size)]], axis=1)
        both = dot(x[:, lanes(r, size)], right, TN).astype(BF16)
        out[0, 0, b] = both[:, :size]
        out[0, 1, b] = both[:, size:]

    for_blocks(ids, pl.program_id(0) * n, n, body)


def line_sum_kernel(
    own, other, rows_in, gain_in, out, rows_out, gain_out, held, below, above, rows_slots, gain_slots,
    pair_send, pair_recv, up_send, up_recv, down_send, down_recv,
    rows_send, rows_recv, gain_send, gain_recv,
):
    chips, arrays, owned = own.shape[:3]
    dp = lax.axis_index("dp")
    tensor = lax.axis_index("tensor")
    chip, core = dp // 2, dp % 2
    sibling = (chip * 2 + 1 - core, tensor)
    upper, lower = (dp + 2, tensor), (dp - 2, tensor)
    has_upper, has_lower = chip < chips - 1, chip > 0
    mesh_id = pl.DeviceIdType.MESH

    dp_count, tensor_count = gain_slots.shape[0], rows_slots.shape[0]

    def dp_peer(k):
        return (lax.rem(dp + k, dp_count), tensor)

    def tensor_peer(k):
        return (dp, lax.rem(tensor + k, tensor_count))

    barrier = pltpu.get_barrier_semaphore()
    for k in range(1, dp_count):
        pl.semaphore_signal(barrier, inc=1, device_id=dp_peer(k), device_id_type=mesh_id)
    for k in range(1, tensor_count):
        pl.semaphore_signal(barrier, inc=1, device_id=tensor_peer(k), device_id_type=mesh_id)
    pl.semaphore_wait(barrier, dp_count + tensor_count - 2)

    def rows_copy(k, slot):
        return pltpu.make_async_remote_copy(
            src_ref=rows_in, dst_ref=rows_slots.at[slot],
            send_sem=rows_send.at[k - 1], recv_sem=rows_recv.at[k - 1],
            device_id=tensor_peer(k), device_id_type=mesh_id,
        )

    def gain_copy(k, slot):
        return pltpu.make_async_remote_copy(
            src_ref=gain_slots.at[dp], dst_ref=gain_slots.at[slot],
            send_sem=gain_send.at[k - 1], recv_sem=gain_recv.at[k - 1],
            device_id=dp_peer(k), device_id_type=mesh_id,
        )

    def rows_sum():
        rows_slots[tensor] = rows_in[...]
        for k in range(1, tensor_count):
            rows_copy(k, lax.rem(tensor - k + tensor_count, tensor_count)).wait_recv()
        total = rows_slots[0]
        for t in range(1, tensor_count):
            total = total + rows_slots[t]
        rows_out[...] = total
        depth_row = gain_in.shape[0] - 8
        gain_slots[dp] = gain_in[...]
        gain_slots[dp, depth_row : depth_row + 1, :] = total[0:1, :]
        for k in range(1, dp_count):
            gain_copy(k, dp).start()

    def gain_sum():
        for k in range(1, dp_count):
            gain_copy(k, lax.rem(dp - k + dp_count, dp_count)).wait_recv()
        total = gain_slots[0]
        for d in range(1, dp_count):
            total = total + gain_slots[d]
        gain_out[...] = total
        for k in range(1, dp_count):
            gain_copy(k, dp).wait_send()
        for k in range(1, tensor_count):
            rows_copy(k, tensor).wait_send()

    def pair_copy(j, a):
        return pltpu.make_async_remote_copy(
            src_ref=other.at[j, a], dst_ref=held.at[j, a],
            send_sem=pair_send.at[j, a], recv_sem=pair_recv.at[j, a],
            device_id=sibling, device_id_type=mesh_id,
        )

    def up_copy(step, a):
        return pltpu.make_async_remote_copy(
            src_ref=held.at[lax.rem(chips - 1 - step + chip, chips), a], dst_ref=below.at[step, a],
            send_sem=up_send.at[step, a], recv_sem=up_recv.at[step, a],
            device_id=upper, device_id_type=mesh_id,
        )

    def down_copy(step, a):
        return pltpu.make_async_remote_copy(
            src_ref=held.at[lax.rem(chip + 1 + step, chips), a], dst_ref=above.at[step, a],
            send_sem=down_send.at[step, a], recv_sem=down_recv.at[step, a],
            device_id=lower, device_id_type=mesh_id,
        )

    for k in range(chips):
        j = jnp.where(2 * chip < chips, chips - 1 - k, k)
        for a in range(arrays):
            pair_copy(j, a).start()

    for k in range(1, tensor_count):
        rows_copy(k, tensor).start()

    def add(j, a, arrived):
        def body(b, carry):
            total = own[j, a, b].astype(F32) + held[j, a, b].astype(F32)
            if arrived is not None:
                total = total + arrived[b].astype(F32)
            held[j, a, b] = total.astype(BF16)
            return carry

        lax.fori_loop(0, owned, body, 0)

    def pass_on(step, a, sends, first, j, copy, arrived):
        @pl.when(sends)
        def _():
            pair_copy(j, a).wait_recv()

            @pl.when(first)
            def _():
                add(j, a, None)

            if step:

                @pl.when(jnp.logical_not(first))
                def _():
                    copy(step - 1, a).wait_recv()
                    add(j, a, arrived.at[step - 1, a])

                @pl.when(sends_at(step - 1, first, chip, copy))
                def _():
                    copy(step - 1, a).wait_send()

            copy(step, a).start()

    def sends_at(step, first, chip, copy):
        return chip <= step if copy is up_copy else chips - 1 - chip <= step

    for step in range(chips - 1):
        for a in range(arrays):
            pass_on(
                step, a, jnp.logical_and(has_upper, chip <= step), chip == 0,
                lax.rem(chips - 1 - step + chip, chips), up_copy, below,
            )
            pass_on(
                step, a, jnp.logical_and(has_lower, chips - 1 - chip <= step), chip == chips - 1,
                lax.rem(chip + 1 + step, chips), down_copy, above,
            )
        if step == 0:
            rows_sum()

    gain_sum()
    for a in range(arrays):
        pair_copy(chip, a).wait_recv()

        @pl.when(has_lower)
        def _():
            up_copy(chips - 2, a).wait_recv()

        @pl.when(has_upper)
        def _():
            down_copy(chips - 2, a).wait_recv()

        def base(b):
            return own[chip, a, b].astype(F32) + held[chip, a, b].astype(F32)

        def each(value):
            def body(b, carry):
                out[a, b] = value(b)
                return carry

            lax.fori_loop(0, owned, body, 0)

        inner = jnp.logical_and(has_lower, has_upper)

        @pl.when(inner)
        def _():
            each(lambda b: base(b) + below[chips - 2, a, b].astype(F32) + above[chips - 2, a, b].astype(F32))

        @pl.when(jnp.logical_and(has_lower, jnp.logical_not(has_upper)))
        def _():
            each(lambda b: base(b) + below[chips - 2, a, b].astype(F32))

        @pl.when(jnp.logical_and(has_upper, jnp.logical_not(has_lower)))
        def _():
            each(lambda b: base(b) + above[chips - 2, a, b].astype(F32))

        for j in range(chips):
            pair_copy(j, a).wait_send()

        @pl.when(has_upper)
        def _():
            up_copy(chips - 2, a).wait_send()

        @pl.when(has_lower)
        def _():
            down_copy(chips - 2, a).wait_send()


def line_sum(own, other, rows, gains):
    chips, arrays = own.shape[:2]
    piece = own.shape[2:]
    line = (chips - 1, arrays)
    tensor_count, dp_count = lax.axis_size("tensor"), 2 * chips
    whole = pl.BlockSpec(memory_space=pltpu.VMEM)
    dma = pltpu.SemaphoreType.DMA
    return pl.pallas_call(
        line_sum_kernel,
        out_shape=[
            jax.ShapeDtypeStruct(own.shape[1:], F32),
            jax.ShapeDtypeStruct(rows.shape, F32),
            jax.ShapeDtypeStruct(gains.shape, F32),
        ],
        in_specs=[whole] * 4,
        out_specs=[whole] * 3,
        scratch_shapes=[
            pltpu.VMEM(own.shape, BF16),
            pltpu.VMEM((*line, *piece), BF16),
            pltpu.VMEM((*line, *piece), BF16),
            pltpu.VMEM((tensor_count, *rows.shape), F32),
            pltpu.VMEM((dp_count, *gains.shape), F32),
            dma((chips, arrays)),
            dma((chips, arrays)),
            dma(line),
            dma(line),
            dma(line),
            dma(line),
            dma((tensor_count - 1,)),
            dma((tensor_count - 1,)),
            dma((dp_count - 1,)),
            dma((dp_count - 1,)),
        ],
        compiler_params=pltpu.CompilerParams(
            collective_id=0, has_side_effects=True, vmem_limit_bytes=56 * 2**20
        ),
        cost_estimate=pl.CostEstimate(
            flops=own.size, bytes_accessed=64 * own.size, transcendentals=0
        ),
        name="gate_up_line",
    )(own, other, rows, gains)


def call(kernel, ids, whole, blocks, outs, flops, steps, acc=None, name=None, after=()):
    read = 1 + len(whole) + len(blocks)

    def body(*refs):
        kernel(*refs[:read], *refs[read + len(after) :])

    chunked = lambda shape: pl.BlockSpec(
        (shape[0] // steps, *shape[1:]), lambda i, ids: (i, *[0] * (len(shape) - 1))
    )
    resident = lambda shape: pl.BlockSpec(shape, lambda i, ids: (0, 0))
    order = [(a, resident(a.shape)) if a.ndim == 2 else (a, chunked(a.shape)) for a in (*whole, *blocks)]
    out_specs = [chunked(s) if cut else resident(s) for s, _, cut in outs]
    out_shape = [jax.ShapeDtypeStruct(s, d) for s, d, _ in outs]
    moved = sum(a.size * a.dtype.itemsize for a, _ in order)
    moved += sum(s.size * s.dtype.itemsize for s in out_shape)
    return pl.pallas_call(
        body,
        out_shape=out_shape,
        grid_spec=pltpu.PrefetchScalarGridSpec(
            num_scalar_prefetch=1,
            grid=(steps,),
            in_specs=[s for _, s in order] + [pl.BlockSpec(memory_space=pl.ANY)] * len(after),
            out_specs=out_specs,
            scratch_shapes=[pltpu.VMEM(acc, F32)] if acc else [],
        ),
        compiler_params=pltpu.CompilerParams(vmem_limit_bytes=60 * 2**20),
        cost_estimate=pl.CostEstimate(flops=4 * flops, bytes_accessed=moved, transcendentals=0),
        name=name,
    )(ids, *[a for a, _ in order], *after)


def per_device(
    history,
    depth_weights,
    depth_index,
    gain,
    gate_blocks,
    up_blocks,
    down_blocks,
    block_ids,
    grad_out,
):
    tokens, width = grad_out.shape
    owned, size = gate_blocks.shape[:2]
    tensor_count = lax.axis_size("tensor")
    dp_count = lax.axis_size("dp")
    chips = dp_count // 2
    hidden_width = FF // tensor_count
    share_width = width // tensor_count
    share_start = lax.axis_index("tensor") * share_width
    dp = lax.axis_index("dp")
    chip, core = dp // 2, dp % 2
    active = block_ids.shape[0]
    ids = block_ids.reshape(-1)
    flops = 2 * active * size * size * tokens

    gate_all = lax.all_gather(gate_blocks, "dp", axis=0, tiled=True)
    up_all = lax.all_gather(up_blocks, "dp", axis=0, tiled=True)
    down_all = lax.all_gather(down_blocks, "dp", axis=0, tiled=True)

    def share(a):
        return lax.dynamic_slice_in_dim(a, share_start, share_width, a.ndim - 1)

    mixed = jnp.zeros((tokens, width), F32)
    for slot in range(depth_index.shape[0]):
        earlier = lax.dynamic_index_in_dim(history, depth_index[slot], 0, keepdims=False)
        mixed = mixed + depth_weights[slot] * earlier.astype(F32)
    scale_inv = lax.rsqrt(jnp.mean(mixed * mixed, axis=-1, keepdims=True) + EPSILON)
    normed = (mixed * scale_inv * gain).astype(BF16)

    cubed = scale_inv * scale_inv * scale_inv / width
    history_share, second = [], []
    for slot in range(depth_index.shape[0]):
        earlier = lax.dynamic_index_in_dim(history, depth_index[slot], 0, keepdims=False)
        history_share.append(share(earlier))
        second.append(jnp.sum(mixed * earlier.astype(F32), axis=-1) * cubed[:, 0])
    history_share, second = jnp.stack(history_share), jnp.stack(second)
    mixed_share = share(mixed)

    acts = (tokens, hidden_width)
    (gate_pre,) = call(
        gate_kernel, ids, [normed], [gate_all], [(acts, F32, False)], flops, CHUNKS, name="gate",
        after=[history_share, second, mixed_share],
    )
    up_pre, hidden = call(
        up_kernel, ids, [normed], [up_all, gate_pre], [(acts, F32, False), (acts, BF16, False)],
        flops, CHUNKS, name="up_hidden",
    )

    owner_ids = block_ids.reshape(chips, 2, owned, 2)

    def half_ids(which):
        return lax.dynamic_index_in_dim(owner_ids, which, 1, keepdims=False).reshape(-1)

    other_ids, own_ids = half_ids(1 - core), half_ids(core)

    siblings = [(i, i ^ 1) for i in range(dp_count)]

    def down_grads(which, after=()):
        (out,) = call(
            down_grad_kernel, which, [hidden, grad_out], [], [((chips, 1, owned, size, size), BF16, True)],
            flops // 2, chips, name="down_grad", after=after,
        )
        return out

    def permute_sum(own, received):
        own = own.reshape(chips, owned, size, size)
        received = received.reshape(chips, owned, size, size)

        def part(target):
            target = jnp.clip(target, 0, chips - 1)
            a = lax.dynamic_index_in_dim(own, target, 0, keepdims=False)
            b = lax.dynamic_index_in_dim(received, target, 0, keepdims=False)
            return a.astype(F32) + b.astype(F32)

        from_below = from_above = None
        for step in range(chips - 1):
            reach = chips - 1 - step
            upward, downward = part(chip + reach), part(chip - reach)
            if step:
                upward = upward + from_below.astype(F32)
                downward = downward + from_above.astype(F32)
            upward, downward = upward.astype(BF16), downward.astype(BF16)
            pairs = [(z, z + 1) for z in range(step + 1)]
            up_pairs = [(2 * a + c, 2 * b + c) for a, b in pairs for c in (0, 1)]
            down_pairs = [
                (2 * (chips - 1 - a) + c, 2 * (chips - 1 - b) + c) for a, b in pairs for c in (0, 1)
            ]
            from_below = lax.ppermute(upward, "dp", up_pairs)
            from_above = lax.ppermute(downward, "dp", down_pairs)
            yield [upward, downward]
        total = part(chip)
        if from_below is not None:
            total = total + from_below.astype(F32) + from_above.astype(F32)
        yield total

    down_other = down_grads(other_ids)
    down_received = lax.ppermute(down_other, "dp", siblings)
    down_own = down_grads(own_ids, [down_other])
    down_line = list(permute_sum(down_own, down_received))
    grad_down = down_line[-1]

    dgate, dup = call(
        hidden_grad_kernel, ids, [grad_out], [down_all, gate_pre, up_pre],
        [(acts, BF16, False), (acts, BF16, False)], flops, CHUNKS, acc=acts, name="hidden_grad",
        after=down_line[min(1, chips - 2)] if chips > 1 else (),
    )

    rows = (tokens, width)
    (normed_grad,) = call(
        normed_grad_kernel, ids, [dgate, dup], [gate_all, up_all], [(rows, BF16, False)],
        2 * flops, CHUNKS, acc=rows, name="normed_grad",
    )
    (ffn,) = call(
        ffn_kernel, ids, [hidden], [down_all], [(rows, BF16, False)], flops, CHUNKS, acc=rows, name="ffn",
        after=[normed_grad, *(down_line[-2] if chips > 1 else ())],
    )

    def gate_up_grads(which):
        (out,) = call(
            gate_up_grad_kernel, which, [normed, dgate, dup], [],
            [((chips, 2, owned, size, size), BF16, True)],
            flops, chips, name="gate_up_grad", after=[ffn],
        )
        return out

    grad_share = lax.psum_scatter(normed_grad, "tensor", scatter_dimension=1, tiled=True).astype(F32)
    ffn_share = lax.psum_scatter(ffn, "tensor", scatter_dimension=1, tiled=True).astype(F32)

    gain_share = share(gain)
    direct = share(grad_out).astype(F32) + scale_inv * gain_share * grad_share
    along_part = jnp.sum(grad_share * gain_share * mixed_share, axis=-1)
    gain_part = jnp.sum(grad_share * mixed_share * scale_inv, axis=0)
    depth_part = jnp.sum(direct * history_share.astype(F32), axis=(1, 2)) - jnp.sum(along_part * second, axis=1)
    slots = depth_index.shape[0]
    token_rows, gain_rows = -(-tokens // 128), -(-share_width // 1024) * 8
    sum_rows = -(-(token_rows + 1) // 8) * 8
    row_terms = jnp.zeros((sum_rows * 128,), F32)
    row_terms = lax.dynamic_update_slice_in_dim(row_terms, depth_part, 0, 0)
    row_terms = lax.dynamic_update_slice_in_dim(row_terms, along_part, 128, 0).reshape(sum_rows, 128)
    gain_terms = jnp.zeros(((gain_rows + 8) * 128,), F32)
    gain_terms = lax.dynamic_update_slice_in_dim(gain_terms, gain_part, 0, 0).reshape(gain_rows + 8, 128)

    block_grads, row_sums, gain_sums = line_sum(
        gate_up_grads(own_ids), gate_up_grads(other_ids), row_terms, gain_terms
    )
    grad_gate, grad_up = block_grads
    depth_sum = gain_sums[gain_rows, :slots]
    gain_sum = gain_sums.reshape(-1)[:share_width]
    along = row_sums.reshape(-1)[128 : 128 + tokens][:, None]
    layer_out = (mixed_share + ffn_share).astype(BF16)
    grad_mixed = direct - mixed_share * cubed * along
    return (layer_out, grad_mixed, grad_gate, grad_up, grad_down, depth_sum, gain_sum)


def solution(mesh):
    placed = (
        P(None, "dp", None),
        P(),
        P(),
        P(),
        P(("tensor", "dp"), None, None),
        P(("tensor", "dp"), None, None),
        P(("tensor", "dp"), None, None),
        P("tensor", None),
        P("dp", None),
    )
    return jax.shard_map(
        per_device,
        mesh=mesh,
        in_specs=placed,
        out_specs=(
            P("dp", "tensor"),
            P("dp", "tensor"),
            P(("tensor", "dp"), None, None),
            P(("tensor", "dp"), None, None),
            P(("tensor", "dp"), None, None),
            P(),
            P("tensor"),
        ),
        check_vma=False,
    )
```

```python
import jax
import jax.numpy as jnp
from jax import lax
from jax.experimental import pallas as pl
from jax.experimental.pallas import tpu as pltpu
from jax.sharding import PartitionSpec as P

FF = 14336
EPSILON = 1e-05
CHUNKS = 8
UNROLL = 7
F32 = jnp.float32
BF16 = jnp.bfloat16
NN = (((1,), (0,)), ((), ()))
NT = (((1,), (1,)), ((), ()))
TN = (((0,), (0,)), ((), ()))


def dot(a, b, dims):
    return lax.dot_general(a, b, dims, preferred_element_type=F32)


def lanes(index, size):
    return pl.ds(pl.multiple_of(index * size, size), size)


def for_blocks(ids, first, count, body):
    def step(i, carry):
        for u in range(UNROLL):
            b = i * UNROLL + u
            body(b, ids[2 * (first + b)], ids[2 * (first + b) + 1])
        return carry

    lax.fori_loop(0, count // UNROLL, step, 0)


def for_columns(size, width, body):
    def step(c, carry):
        body(lanes(c, size))
        return carry

    lax.fori_loop(0, width // size, step, 0)


def gate_kernel(ids, x, w, acc):
    n, size = w.shape[0], w.shape[1]

    @pl.when(pl.program_id(0) == 0)
    def _():
        acc[...] = jnp.zeros_like(acc)

    def body(b, r, c):
        acc[:, lanes(c, size)] += dot(x[:, lanes(r, size)], w[b], NN)

    for_blocks(ids, pl.program_id(0) * n, n, body)


def up_kernel(ids, x, w, gate, acc, hidden):
    n, size = w.shape[0], w.shape[1]
    gate_kernel(ids, x, w, acc)

    @pl.when(pl.program_id(0) == pl.num_programs(0) - 1)
    def _():
        def body(cols):
            g = gate[:, cols]
            hidden[:, cols] = (g / (1.0 + jnp.exp(-g)) * acc[:, cols]).astype(BF16)

        for_columns(size, acc.shape[1], body)


def hidden_grad_kernel(ids, gout, w, gate, up, dgate, dup, acc):
    n, size = w.shape[0], w.shape[1]

    @pl.when(pl.program_id(0) == 0)
    def _():
        acc[...] = jnp.zeros_like(acc)

    def body(b, r, c):
        acc[:, lanes(c, size)] += dot(gout[:, lanes(r, size)], w[b], NT)

    for_blocks(ids, pl.program_id(0) * n, n, body)

    @pl.when(pl.program_id(0) == pl.num_programs(0) - 1)
    def _():
        def finish(cols):
            g = gate[:, cols]
            s = 1.0 / (1.0 + jnp.exp(-g))
            gh = acc[:, cols]
            dgate[:, cols] = (gh * up[:, cols] * s * (1.0 + g * (1.0 - s))).astype(BF16)
            dup[:, cols] = (gh * g * s).astype(BF16)

        for_columns(size, acc.shape[1], finish)


def ffn_kernel(ids, hidden, w, out, acc):
    n, size = w.shape[0], w.shape[1]

    @pl.when(pl.program_id(0) == 0)
    def _():
        acc[...] = jnp.zeros_like(acc)

    def body(b, r, c):
        acc[:, lanes(r, size)] += dot(hidden[:, lanes(c, size)], w[b], NN)

    for_blocks(ids, pl.program_id(0) * n, n, body)

    @pl.when(pl.program_id(0) == pl.num_programs(0) - 1)
    def _():
        out[...] = acc[...].astype(BF16)


def normed_grad_kernel(ids, dgate, dup, gate_w, up_w, out, acc):
    n, size = gate_w.shape[0], gate_w.shape[1]

    @pl.when(pl.program_id(0) == 0)
    def _():
        acc[...] = jnp.zeros_like(acc)

    def body(b, r, c):
        left = jnp.concatenate([dgate[:, lanes(c, size)], dup[:, lanes(c, size)]], axis=1)
        right = jnp.concatenate([gate_w[b], up_w[b]], axis=1)
        acc[:, lanes(r, size)] += dot(left, right, NT)

    for_blocks(ids, pl.program_id(0) * n, n, body)

    @pl.when(pl.program_id(0) == pl.num_programs(0) - 1)
    def _():
        out[...] = acc[...].astype(BF16)


def down_grad_kernel(ids, hidden, gout, out):
    n, size = out.shape[2], out.shape[3]

    def body(b, r, c):
        out[0, 0, b] = dot(hidden[:, lanes(c, size)], gout[:, lanes(r, size)], TN).astype(BF16)

    for_blocks(ids, pl.program_id(0) * n, n, body)


def gate_up_grad_kernel(ids, x, dgate, dup, out):
    n, size = out.shape[2], out.shape[3]

    def body(b, r, c):
        right = jnp.concatenate([dgate[:, lanes(c, size)], dup[:, lanes(c, size)]], axis=1)
        both = dot(x[:, lanes(r, size)], right, TN).astype(BF16)
        out[0, 0, b] = both[:, :size]
        out[0, 1, b] = both[:, size:]

    for_blocks(ids, pl.program_id(0) * n, n, body)


def line_sum_kernel(
    own, other, rows_in, gain_in, out_gate, out_up, rows_out, gain_out, held, below, above, rows_slots, gain_slots,
    pair_send, pair_recv, up_send, up_recv, down_send, down_recv,
    rows_send, rows_recv, gain_send, gain_recv,
):
    chips, arrays, owned = own.shape[:3]
    dp = lax.axis_index("dp")
    tensor = lax.axis_index("tensor")
    chip, core = dp // 2, dp % 2
    sibling = (chip * 2 + 1 - core, tensor)
    upper, lower = (dp + 2, tensor), (dp - 2, tensor)
    has_upper, has_lower = chip < chips - 1, chip > 0
    mesh_id = pl.DeviceIdType.MESH

    dp_count, tensor_count = gain_slots.shape[0], rows_slots.shape[0]

    def dp_peer(k):
        return (lax.rem(dp + k, dp_count), tensor)

    def tensor_peer(k):
        return (dp, lax.rem(tensor + k, tensor_count))

    barrier = pltpu.get_barrier_semaphore()
    for k in range(1, dp_count):
        pl.semaphore_signal(barrier, inc=1, device_id=dp_peer(k), device_id_type=mesh_id)
    for k in range(1, tensor_count):
        pl.semaphore_signal(barrier, inc=1, device_id=tensor_peer(k), device_id_type=mesh_id)
    pl.semaphore_wait(barrier, dp_count + tensor_count - 2)

    def rows_copy(k, slot):
        return pltpu.make_async_remote_copy(
            src_ref=rows_in, dst_ref=rows_slots.at[slot],
            send_sem=rows_send.at[k - 1], recv_sem=rows_recv.at[k - 1],
            device_id=tensor_peer(k), device_id_type=mesh_id,
        )

    def gain_copy(k, slot):
        return pltpu.make_async_remote_copy(
            src_ref=gain_slots.at[dp], dst_ref=gain_slots.at[slot],
            send_sem=gain_send.at[k - 1], recv_sem=gain_recv.at[k - 1],
            device_id=dp_peer(k), device_id_type=mesh_id,
        )

    def rows_sum():
        rows_slots[tensor] = rows_in[...]
        for k in range(1, tensor_count):
            rows_copy(k, lax.rem(tensor - k + tensor_count, tensor_count)).wait_recv()
        total = rows_slots[0]
        for t in range(1, tensor_count):
            total = total + rows_slots[t]
        rows_out[...] = total
        depth_row = gain_in.shape[0] - 8
        gain_slots[dp] = gain_in[...]
        gain_slots[dp, depth_row : depth_row + 1, :] = total[0:1, :]
        for k in range(1, dp_count):
            gain_copy(k, dp).start()

    def gain_sum():
        for k in range(1, dp_count):
            gain_copy(k, lax.rem(dp - k + dp_count, dp_count)).wait_recv()
        total = gain_slots[0]
        for d in range(1, dp_count):
            total = total + gain_slots[d]
        gain_out[...] = total
        for k in range(1, dp_count):
            gain_copy(k, dp).wait_send()
        for k in range(1, tensor_count):
            rows_copy(k, tensor).wait_send()

    def pair_copy(j, a):
        return pltpu.make_async_remote_copy(
            src_ref=other.at[j, a], dst_ref=held.at[j, a],
            send_sem=pair_send.at[j, a], recv_sem=pair_recv.at[j, a],
            device_id=sibling, device_id_type=mesh_id,
        )

    def up_copy(step, a):
        return pltpu.make_async_remote_copy(
            src_ref=held.at[lax.rem(chips - 1 - step + chip, chips), a], dst_ref=below.at[step, a],
            send_sem=up_send.at[step, a], recv_sem=up_recv.at[step, a],
            device_id=upper, device_id_type=mesh_id,
        )

    def down_copy(step, a):
        return pltpu.make_async_remote_copy(
            src_ref=held.at[lax.rem(chip + 1 + step, chips), a], dst_ref=above.at[step, a],
            send_sem=down_send.at[step, a], recv_sem=down_recv.at[step, a],
            device_id=lower, device_id_type=mesh_id,
        )

    for k in range(chips):
        j = jnp.where(2 * chip < chips, chips - 1 - k, k)
        for a in range(arrays):
            pair_copy(j, a).start()

    for k in range(1, tensor_count):
        rows_copy(k, tensor).start()

    def add(j, a, arrived):
        def body(b, carry):
            total = own[j, a, b].astype(F32) + held[j, a, b].astype(F32)
            if arrived is not None:
                total = total + arrived[b].astype(F32)
            held[j, a, b] = total.astype(BF16)
            return carry

        lax.fori_loop(0, owned, body, 0)

    def pass_on(step, a, sends, first, j, copy, arrived):
        @pl.when(sends)
        def _():
            pair_copy(j, a).wait_recv()

            @pl.when(first)
            def _():
                add(j, a, None)

            if step:

                @pl.when(jnp.logical_not(first))
                def _():
                    copy(step - 1, a).wait_recv()
                    add(j, a, arrived.at[step - 1, a])

                @pl.when(sends_at(step - 1, first, chip, copy))
                def _():
                    copy(step - 1, a).wait_send()

            copy(step, a).start()

    def sends_at(step, first, chip, copy):
        return chip <= step if copy is up_copy else chips - 1 - chip <= step

    for step in range(chips - 1):
        for a in range(arrays):
            pass_on(
                step, a, jnp.logical_and(has_upper, chip <= step), chip == 0,
                lax.rem(chips - 1 - step + chip, chips), up_copy, below,
            )
            pass_on(
                step, a, jnp.logical_and(has_lower, chips - 1 - chip <= step), chip == chips - 1,
                lax.rem(chip + 1 + step, chips), down_copy, above,
            )
        if step == 0:
            rows_sum()

    gain_sum()
    for a in range(arrays):
        pair_copy(chip, a).wait_recv()

        @pl.when(has_lower)
        def _():
            up_copy(chips - 2, a).wait_recv()

        @pl.when(has_upper)
        def _():
            down_copy(chips - 2, a).wait_recv()

        def base(b):
            return own[chip, a, b].astype(F32) + held[chip, a, b].astype(F32)

        def each(value):
            def body(b, carry):
                (out_gate, out_up)[a][b] = value(b)
                return carry

            lax.fori_loop(0, owned, body, 0)

        inner = jnp.logical_and(has_lower, has_upper)

        @pl.when(inner)
        def _():
            each(lambda b: base(b) + below[chips - 2, a, b].astype(F32) + above[chips - 2, a, b].astype(F32))

        @pl.when(jnp.logical_and(has_lower, jnp.logical_not(has_upper)))
        def _():
            each(lambda b: base(b) + below[chips - 2, a, b].astype(F32))

        @pl.when(jnp.logical_and(has_upper, jnp.logical_not(has_lower)))
        def _():
            each(lambda b: base(b) + above[chips - 2, a, b].astype(F32))

        for j in range(chips):
            pair_copy(j, a).wait_send()

        @pl.when(has_upper)
        def _():
            up_copy(chips - 2, a).wait_send()

        @pl.when(has_lower)
        def _():
            down_copy(chips - 2, a).wait_send()


def line_sum(own, other, rows, gains):
    chips, arrays = own.shape[:2]
    piece = own.shape[2:]
    line = (chips - 1, arrays)
    tensor_count, dp_count = lax.axis_size("tensor"), 2 * chips
    whole = pl.BlockSpec(memory_space=pltpu.VMEM)
    dma = pltpu.SemaphoreType.DMA
    return pl.pallas_call(
        line_sum_kernel,
        out_shape=[
            jax.ShapeDtypeStruct(piece, F32),
            jax.ShapeDtypeStruct(piece, F32),
            jax.ShapeDtypeStruct(rows.shape, F32),
            jax.ShapeDtypeStruct(gains.shape, F32),
        ],
        in_specs=[whole] * 4,
        out_specs=[whole] * 4,
        scratch_shapes=[
            pltpu.VMEM(own.shape, BF16),
            pltpu.VMEM((*line, *piece), BF16),
            pltpu.VMEM((*line, *piece), BF16),
            pltpu.VMEM((tensor_count, *rows.shape), F32),
            pltpu.VMEM((dp_count, *gains.shape), F32),
            dma((chips, arrays)),
            dma((chips, arrays)),
            dma(line),
            dma(line),
            dma(line),
            dma(line),
            dma((tensor_count - 1,)),
            dma((tensor_count - 1,)),
            dma((dp_count - 1,)),
            dma((dp_count - 1,)),
        ],
        compiler_params=pltpu.CompilerParams(
            collective_id=0, has_side_effects=True, vmem_limit_bytes=56 * 2**20
        ),
        cost_estimate=pl.CostEstimate(
            flops=own.size, bytes_accessed=64 * own.size, transcendentals=0
        ),
        name="gate_up_line",
    )(own, other, rows, gains)


def call(kernel, ids, whole, blocks, outs, flops, steps, acc=None, name=None, after=()):
    read = 1 + len(whole) + len(blocks)

    def body(*refs):
        kernel(*refs[:read], *refs[read + len(after) :])

    chunked = lambda shape: pl.BlockSpec(
        (shape[0] // steps, *shape[1:]), lambda i, ids: (i, *[0] * (len(shape) - 1))
    )
    resident = lambda shape: pl.BlockSpec(shape, lambda i, ids: (0, 0))
    order = [(a, resident(a.shape)) if a.ndim == 2 else (a, chunked(a.shape)) for a in (*whole, *blocks)]
    out_specs = [chunked(s) if cut else resident(s) for s, _, cut in outs]
    out_shape = [jax.ShapeDtypeStruct(s, d) for s, d, _ in outs]
    moved = sum(a.size * a.dtype.itemsize for a, _ in order)
    moved += sum(s.size * s.dtype.itemsize for s in out_shape)
    return pl.pallas_call(
        body,
        out_shape=out_shape,
        grid_spec=pltpu.PrefetchScalarGridSpec(
            num_scalar_prefetch=1,
            grid=(steps,),
            in_specs=[s for _, s in order] + [pl.BlockSpec(memory_space=pl.ANY)] * len(after),
            out_specs=out_specs,
            scratch_shapes=[pltpu.VMEM(acc, F32)] if acc else [],
        ),
        compiler_params=pltpu.CompilerParams(vmem_limit_bytes=40 * 2**20),
        cost_estimate=pl.CostEstimate(flops=4 * flops, bytes_accessed=moved, transcendentals=0),
        name=name,
    )(ids, *[a for a, _ in order], *after)


def per_device(
    history,
    depth_weights,
    depth_index,
    gain,
    gate_blocks,
    up_blocks,
    down_blocks,
    block_ids,
    grad_out,
):
    tokens, width = grad_out.shape
    owned, size = gate_blocks.shape[:2]
    tensor_count = lax.axis_size("tensor")
    dp_count = lax.axis_size("dp")
    chips = dp_count // 2
    hidden_width = FF // tensor_count
    share_width = width // tensor_count
    share_start = lax.axis_index("tensor") * share_width
    dp = lax.axis_index("dp")
    chip, core = dp // 2, dp % 2
    active = block_ids.shape[0]
    ids = block_ids.reshape(-1)
    flops = 2 * active * size * size * tokens

    gate_all = lax.all_gather(gate_blocks, "dp", axis=0, tiled=True)
    up_all = lax.all_gather(up_blocks, "dp", axis=0, tiled=True)
    down_all = lax.all_gather(down_blocks, "dp", axis=0, tiled=True)

    def share(a):
        return lax.dynamic_slice_in_dim(a, share_start, share_width, a.ndim - 1)

    mixed = jnp.zeros((tokens, width), F32)
    for slot in range(depth_index.shape[0]):
        earlier = lax.dynamic_index_in_dim(history, depth_index[slot], 0, keepdims=False)
        mixed = mixed + depth_weights[slot] * earlier.astype(F32)
    scale_inv = lax.rsqrt(jnp.mean(mixed * mixed, axis=-1, keepdims=True) + EPSILON)
    normed = (mixed * scale_inv * gain).astype(BF16)

    cubed = scale_inv * scale_inv * scale_inv / width
    history_share, second = [], []
    for slot in range(depth_index.shape[0]):
        earlier = lax.dynamic_index_in_dim(history, depth_index[slot], 0, keepdims=False)
        history_share.append(share(earlier))
        second.append(jnp.sum(mixed * earlier.astype(F32), axis=-1) * cubed[:, 0])
    history_share, second = jnp.stack(history_share), jnp.stack(second)
    mixed_share = share(mixed)

    acts = (tokens, hidden_width)
    (gate_pre,) = call(
        gate_kernel, ids, [normed], [gate_all], [(acts, F32, False)], flops, CHUNKS, name="gate",
        after=[history_share, second, mixed_share],
    )
    up_pre, hidden = call(
        up_kernel, ids, [normed], [up_all, gate_pre], [(acts, F32, False), (acts, BF16, False)],
        flops, CHUNKS, name="up_hidden",
    )

    owner_ids = block_ids.reshape(chips, 2, owned, 2)

    def half_ids(which):
        return lax.dynamic_index_in_dim(owner_ids, which, 1, keepdims=False).reshape(-1)

    other_ids, own_ids = half_ids(1 - core), half_ids(core)

    siblings = [(i, i ^ 1) for i in range(dp_count)]

    def down_grads(which, after=()):
        (out,) = call(
            down_grad_kernel, which, [hidden, grad_out], [], [((chips, 1, owned, size, size), BF16, True)],
            flops // 2, chips, name="down_grad", after=after,
        )
        return out

    def permute_sum(own, received):
        own = own.reshape(chips, owned, size, size)
        received = received.reshape(chips, owned, size, size)

        def part(target):
            target = jnp.clip(target, 0, chips - 1)
            a = lax.dynamic_index_in_dim(own, target, 0, keepdims=False)
            b = lax.dynamic_index_in_dim(received, target, 0, keepdims=False)
            return a.astype(F32) + b.astype(F32)

        from_below = from_above = None
        for step in range(chips - 1):
            reach = chips - 1 - step
            upward, downward = part(chip + reach), part(chip - reach)
            if step:
                upward = upward + from_below.astype(F32)
                downward = downward + from_above.astype(F32)
            upward, downward = upward.astype(BF16), downward.astype(BF16)
            pairs = [(z, z + 1) for z in range(step + 1)]
            up_pairs = [(2 * a + c, 2 * b + c) for a, b in pairs for c in (0, 1)]
            down_pairs = [
                (2 * (chips - 1 - a) + c, 2 * (chips - 1 - b) + c) for a, b in pairs for c in (0, 1)
            ]
            from_below = lax.ppermute(upward, "dp", up_pairs)
            from_above = lax.ppermute(downward, "dp", down_pairs)
            yield [upward, downward]
        total = part(chip)
        if from_below is not None:
            total = total + from_below.astype(F32) + from_above.astype(F32)
        yield total

    down_other = down_grads(other_ids)
    down_received = lax.ppermute(down_other, "dp", siblings)
    down_own = down_grads(own_ids, [down_other])
    down_line = list(permute_sum(down_own, down_received))
    grad_down = down_line[-1]

    dgate, dup = call(
        hidden_grad_kernel, ids, [grad_out], [down_all, gate_pre, up_pre],
        [(acts, BF16, False), (acts, BF16, False)], flops, CHUNKS, acc=acts, name="hidden_grad",
        after=down_line[min(1, chips - 2)] if chips > 1 else (),
    )

    rows = (tokens, width)
    (normed_grad,) = call(
        normed_grad_kernel, ids, [dgate, dup], [gate_all, up_all], [(rows, BF16, False)],
        2 * flops, CHUNKS, acc=rows, name="normed_grad",
    )
    (ffn,) = call(
        ffn_kernel, ids, [hidden], [down_all], [(rows, BF16, False)], flops, CHUNKS, acc=rows, name="ffn",
        after=[normed_grad],
    )

    def gate_up_grads(which):
        (out,) = call(
            gate_up_grad_kernel, which, [normed, dgate, dup], [],
            [((chips, 2, owned, size, size), BF16, True)],
            flops, chips, name="gate_up_grad", after=[ffn],
        )
        return out

    grad_share = lax.psum_scatter(normed_grad, "tensor", scatter_dimension=1, tiled=True).astype(F32)
    ffn_share = lax.psum_scatter(ffn, "tensor", scatter_dimension=1, tiled=True).astype(F32)

    gain_share = share(gain)
    direct = share(grad_out).astype(F32) + scale_inv * gain_share * grad_share
    along_part = jnp.sum(grad_share * gain_share * mixed_share, axis=-1)
    gain_part = jnp.sum(grad_share * mixed_share * scale_inv, axis=0)
    depth_part = jnp.sum(direct * history_share.astype(F32), axis=(1, 2)) - jnp.sum(along_part * second, axis=1)
    slots = depth_index.shape[0]
    token_rows, gain_rows = -(-tokens // 128), -(-share_width // 1024) * 8
    sum_rows = -(-(token_rows + 1) // 8) * 8
    row_terms = jnp.zeros((sum_rows * 128,), F32)
    row_terms = lax.dynamic_update_slice_in_dim(row_terms, depth_part, 0, 0)
    row_terms = lax.dynamic_update_slice_in_dim(row_terms, along_part, 128, 0).reshape(sum_rows, 128)
    gain_terms = jnp.zeros(((gain_rows + 8) * 128,), F32)
    gain_terms = lax.dynamic_update_slice_in_dim(gain_terms, gain_part, 0, 0).reshape(gain_rows + 8, 128)

    grad_gate, grad_up, row_sums, gain_sums = line_sum(
        gate_up_grads(own_ids), gate_up_grads(other_ids), row_terms, gain_terms
    )
    depth_sum = gain_sums[gain_rows, :slots]
    gain_sum = gain_sums.reshape(-1)[:share_width]
    along = row_sums.reshape(-1)[128 : 128 + tokens][:, None]
    layer_out = (mixed_share + ffn_share).astype(BF16)
    grad_mixed = direct - mixed_share * cubed * along
    return (layer_out, grad_mixed, grad_gate, grad_up, grad_down, depth_sum, gain_sum)


def solution(mesh):
    placed = (
        P(None, "dp", None),
        P(),
        P(),
        P(),
        P(("tensor", "dp"), None, None),
        P(("tensor", "dp"), None, None),
        P(("tensor", "dp"), None, None),
        P("tensor", None),
        P("dp", None),
    )
    return jax.shard_map(
        per_device,
        mesh=mesh,
        in_specs=placed,
        out_specs=(
            P("dp", "tensor"),
            P("dp", "tensor"),
            P(("tensor", "dp"), None, None),
            P(("tensor", "dp"), None, None),
            P(("tensor", "dp"), None, None),
            P(),
            P("tensor"),
        ),
        check_vma=False,
    )
```
